256 devices in a mesh: pool: 2 (over core), group: 32 (over x, y, z_hi), tensor: 4 (over z_lo).
Axes of the slice: x: 4, y: 4, z: 8 (z_hi: 2, z_lo: 4; z = z_hi * 4 + z_lo), core: 2. Of those that a mesh axis runs over, the one named last changes fastest.
Arguments:
- queries: bfloat16 [2, 6144, 5120], P('pool', 'group', 'tensor'), may hold values from -8 to 8
- new_keys: bfloat16 [2, 6144, 1024], P('pool', 'group', 'tensor'), may hold values from -8 to 8
- new_values: bfloat16 [2, 6144, 1024], P('pool', 'group', 'tensor'), may hold values from -6 to 6
- cache_keys: bfloat16 [2, 32, 4096, 1024], P('pool', 'group', None, 'tensor'), may hold values from -8 to 8
- cache_values: bfloat16 [2, 32, 4096, 1024], P('pool', 'group', None, 'tensor'), may hold values from -6 to 6
- prefix_len: int32 [2, 32], P('pool', 'group'), may hold values from 1 to 4096, as said below
- span_len: int32 [2, 32], P('pool', 'group'), may hold values from 1 to 192, as said below
- residual: bfloat16 [2, 6144, 5120], P('pool', 'group', 'tensor'), may hold values from -60 to 60
- out_proj: bfloat16 [2, 5120, 5120], P('pool', 'tensor', 'group'), may hold values from -1.1953125 to 1.1953125
- norm_gain: float32 [2, 5120], P('pool', 'tensor'), may hold values from 0.5 to 1.5
Outputs:
- stream: bfloat16 [2, 6144, 5120], P('pool', 'group', 'tensor')
- normed: bfloat16 [2, 6144, 5120], P('pool', 'group', 'tensor')
The draws below stay inside these ranges and needn't reach their ends.
Inputs may be any that keep to these rules, and one draw needn't show every extreme that they name: `prefix_len`: in each pool some sequence has exactly 4096 cached tokens. `span_len`: most spans are full; in each pool some span has 192 real tokens.
All inputs are finite; a program needn't handle non-finite values.
Results may differ from the reference program's by a relative error of at most 0.0055.
Values may be sent and summed in bfloat16 or wider, within the bound.
A program may use at most 128 MiB of HBM per device.

```python
import math
import jax
import jax.numpy as jnp
from jax import lax

D = 5120
H = 40
KVH = 8
HD = 128
PREFIX = 4096
SPAN = 192
SEQS = 32
TOKENS = 6144
N_TENSOR = 4


def draw_queries(key, part):
    key = jax.random.fold_in(key, 11)
    values_drawn = 1.2 * jnp.clip(jax.random.normal(key, (2, SEQS, SPAN, H, HD), jnp.float32), -5.0, 5.0)
    return values_drawn.reshape(2, SEQS * SPAN, H * HD).astype(jnp.bfloat16)


def draw_new_keys(key, part):
    key = jax.random.fold_in(key, 23)
    values_drawn = 1.2 * jnp.clip(jax.random.normal(key, (2, SEQS, SPAN, KVH, HD), jnp.float32), -5.0, 5.0)
    return values_drawn.reshape(2, SEQS * SPAN, KVH * HD).astype(jnp.bfloat16)


def draw_cache_keys(key, part):
    key = jax.random.fold_in(key, 37)
    values_drawn = 1.2 * jnp.clip(jax.random.normal(key, (2, SEQS, PREFIX, KVH, HD), jnp.float32), -5.0, 5.0)
    return values_drawn.reshape(2, SEQS, PREFIX, KVH * HD).astype(jnp.bfloat16)


def draw_residual(key, part):
    key = jax.random.fold_in(key, 41)
    row_key, col_key, main_key = jax.random.split(key, 3)
    columns = jnp.arange(D, dtype=jnp.float32) / D
    col_scale = 10.0 ** columns * jax.random.uniform(col_key, (D,), jnp.float32, 0.7, 1.4)
    row_scale = 10.0 ** jax.random.uniform(row_key, (2, TOKENS, 1), jnp.float32)
    values_drawn = jnp.clip(jax.random.normal(main_key, (2, TOKENS, D), jnp.float32), -4.0, 4.0)
    return (0.1 * row_scale * col_scale[None, None, :] * values_drawn).astype(jnp.bfloat16)


def draw_prefix_len(key, part):
    key = jax.random.fold_in(key, 61)
    first, second = jax.random.split(key)
    lengths = jax.random.randint(first, (2, SEQS), 1, PREFIX + 1)
    chosen = jax.random.randint(second, (2,), 0, SEQS)
    return lengths.at[jnp.arange(2), chosen].set(PREFIX).astype(jnp.int32)


def draw_span_len(key, part):
    key = jax.random.fold_in(key, 73)
    first, second, third = jax.random.split(key, 3)
    coin = jax.random.randint(first, (2, SEQS), 0, 4)
    shorter = jax.random.randint(second, (2, SEQS), 1, SPAN + 1)
    lengths = jnp.where(coin < 3, SPAN, shorter)
    chosen = jax.random.randint(third, (2,), 0, SEQS)
    return lengths.at[jnp.arange(2), chosen].set(SPAN).astype(jnp.int32)


def level_of(own_key, dims, pieces, smallest, high):
    level = 1.0
    for axis_at, parts in pieces:
        draws = jax.random.uniform(jax.random.fold_in(jax.random.fold_in(own_key, 6), axis_at), (parts,), jnp.float32, smallest / len(pieces), high / len(pieces))
        level = level * jnp.repeat(jnp.exp(draws), dims[axis_at] // parts).reshape((-1,) + (1,) * (len(dims) - 1 - axis_at))
    return level


def bell_draw(stream_key, extent, width, reach, cuts=(), kind=jnp.bfloat16):
    drawn = width * jax.random.normal(stream_key, extent, jnp.float32)
    if cuts:
        drawn = drawn * level_of(stream_key, extent, cuts, -0.22, 0.18)
    return jnp.clip(drawn, -reach, reach).astype(kind)


def setup_inputs(seed: int = 0) -> dict:
    key_of = jax.random.split(jax.random.key(seed), 11)
    return {
        "queries": draw_queries(jax.random.fold_in(key_of[10], 71), 0),
        "new_keys": draw_new_keys(jax.random.fold_in(key_of[10], 71), 0),
        "new_values": bell_draw(key_of[2], (2, TOKENS, KVH * HD), 1.0, 6.0, ((0, 2), (1, 32), (2, 4))),
        "cache_keys": draw_cache_keys(jax.random.fold_in(key_of[10], 71), 0),
        "cache_values": bell_draw(key_of[4], (2, SEQS, PREFIX, KVH * HD), 1.0, 6.0, ((0, 2), (1, 32), (3, 4))),
        "prefix_len": draw_prefix_len(jax.random.fold_in(key_of[10], 71), 0),
        "span_len": draw_span_len(jax.random.fold_in(key_of[10], 71), 0),
        "residual": draw_residual(jax.random.fold_in(key_of[10], 71), 0),
        "out_proj": bell_draw(key_of[8], (2, H * HD, D), 0.2, 1.1953125, ((0, 2), (1, 4), (2, 32))),
        "norm_gain": jnp.clip(1.0 + 0.1 * jax.random.normal(key_of[9], (2, D), jnp.float32), 0.5, 1.5),
    }


def attend(q_block, prefix_k, prefix_v, span_k, span_v, prefix_count, span_count):
    scaling = 1.0 / math.sqrt(HD)
    q_float = q_block.astype(jnp.float32)
    prefix_scores = jnp.einsum('ingd,knd->ngik', q_float, prefix_k.astype(jnp.float32)) * scaling
    span_scores = jnp.einsum('ingd,knd->ngik', q_float, span_k.astype(jnp.float32)) * scaling
    positions = jnp.arange(PREFIX, dtype=jnp.int32)
    prefix_scores = jnp.where((positions < prefix_count)[None, None, None, :], prefix_scores, -jnp.inf)
    query_pos = jnp.arange(SPAN, dtype=jnp.int32)[:, None]
    key_pos = jnp.arange(SPAN, dtype=jnp.int32)[None, :]
    span_mask = (key_pos <= query_pos) & (key_pos < span_count)
    span_scores = jnp.where(span_mask[None, None], span_scores, -jnp.inf)
    highest = jnp.maximum(prefix_scores.max(axis=-1), span_scores.max(axis=-1))
    prefix_exp = jnp.exp(prefix_scores - highest[..., None])
    span_exp = jnp.exp(span_scores - highest[..., None])
    denominator = prefix_exp.sum(axis=-1) + span_exp.sum(axis=-1)
    prefix_round = lax.optimization_barrier(prefix_exp.astype(jnp.bfloat16)).astype(jnp.float32)
    span_round = lax.optimization_barrier(span_exp.astype(jnp.bfloat16)).astype(jnp.float32)
    numerator = jnp.einsum('ngik,knd->ingd', prefix_round, prefix_v.astype(jnp.float32))
    numerator = numerator + jnp.einsum('ngik,knd->ingd', span_round, span_v.astype(jnp.float32))
    result = numerator / jnp.transpose(denominator, (2, 0, 1))[..., None]
    return result.astype(jnp.bfloat16).reshape(SPAN, H * HD)

def tiled_form(matrix):
    blocks = SEQS // 4
    narrow = D // (4 * N_TENSOR)
    shaped = matrix.reshape(blocks, 4 * SPAN, N_TENSOR, 4, narrow)
    shaped = jnp.transpose(shaped, (0, 3, 2, 1, 4)).reshape(blocks, 4, N_TENSOR, SPAN, 4 * narrow)
    return jnp.transpose(shaped, (0, 1, 3, 2, 4)).reshape(TOKENS, D)

def untiled_form(matrix):
    blocks = SEQS // 4
    narrow = D // (4 * N_TENSOR)
    shaped = matrix.reshape(blocks, 4, SPAN, N_TENSOR, 4 * narrow)
    shaped = jnp.transpose(shaped, (0, 1, 3, 2, 4)).reshape(blocks, 4, N_TENSOR, 4 * SPAN, narrow)
    return jnp.transpose(shaped, (0, 3, 2, 1, 4)).reshape(TOKENS, D)

def normalize(rows_in, gain):
    rows_float = rows_in.astype(jnp.float32)
    mean_square = lax.optimization_barrier(jnp.mean(rows_float * rows_float, axis=-1, keepdims=True))
    return (rows_float * lax.rsqrt(mean_square + 1e-06) * gain[None, :]).astype(jnp.bfloat16)

def reference(queries, new_keys, new_values, cache_keys, cache_values, prefix_len, span_len, residual, out_proj, norm_gain):
    group_heads = H // KVH
    layers = []
    for section in range(2):
        q_all = queries[section].reshape(SEQS, SPAN, KVH, group_heads, HD)
        span_keys = new_keys[section].reshape(SEQS, SPAN, KVH, HD)
        span_values = new_values[section].reshape(SEQS, SPAN, KVH, HD)
        past_keys = cache_keys[section].reshape(SEQS, PREFIX, KVH, HD)
        past_values = cache_values[section].reshape(SEQS, PREFIX, KVH, HD)

        def per_seq(operands):
            return attend(*operands)
        attended = lax.map(per_seq, (q_all, past_keys, past_values, span_keys, span_values, prefix_len[section], span_len[section]))
        attended = attended.reshape(SEQS * SPAN, H * HD)
        projected = jnp.dot(attended, out_proj[section], preferred_element_type=jnp.float32)
        if section == 0:
            stream_in = untiled_form(residual[0])
        else:
            stream_in = residual[1]
        layers.append((stream_in.astype(jnp.float32) + projected).astype(jnp.bfloat16))
    stream = jnp.stack([tiled_form(layers[1]), layers[0]])
    normed = jnp.stack([tiled_form(normalize(layers[1], norm_gain[0])), normalize(layers[0], norm_gain[1])])
    return (stream, normed)
```

```python
import functools
import math

import jax
import jax.numpy as jnp
from jax import lax
from jax.experimental import pallas as pl
from jax.experimental.pallas import tpu as pltpu
from jax.sharding import PartitionSpec as P

D = 5120
HD = 128
KVL = 2
GROUP_HEADS = 5
PREFIX = 4096
SPAN = 192
ROWS = GROUP_HEADS * SPAN
HALF = GROUP_HEADS * HD
EPSILON = 1e-6
KEY_BLOCK = 2048
BLOCKS = PREFIX // KEY_BLOCK
PIECE = 320
WCOLS = 160
LOG2 = math.log2(math.e) / math.sqrt(HD)
MASKED = -1e30
MESH = pl.DeviceIdType.MESH


def nt(a, b, precision=None):
    return lax.dot_general(
        a, b, (((1,), (1,)), ((), ())), preferred_element_type=jnp.float32, precision=precision
    )


def body(
    plen_ref, slen_ref, q_hbm, k_hbm, v_hbm, sk_hbm, sv_hbm, w_hbm, res_hbm, gain_ref,
    stream_hbm, normed_hbm,
    q_ref, k_ref, v_ref, sk_ref, sv_ref,
    qs, S, Sp, mx, acc, va, vas,
    wg, ag, pr, pb, rcv1, s2, rcv2, rres, turn, lb, st, nm, sums,
    in_sem, w_loc, w_zs, w_xs, w_rs, a_ss, a_rs, res_ss, res_rs,
    p1_ss, p1_rs, p2_ss, p2_rs, f_ss, f_rs, q_ss, q_rs, out_sem,
):
    pool = lax.axis_index("pool")
    group = lax.axis_index("group")
    t = lax.axis_index("tensor")
    h = lax.rem(group, 2)
    y = lax.rem(lax.div(group, 2), 4)
    x = lax.div(group, 8)
    ylo = lax.rem(y, 2)
    yhi = lax.div(y, 2)
    zero_pool = pool == 0

    def device(px, xx, yy, hh, tt):
        return (px, (xx * 4 + yy) * 2 + hh, tt)

    def remote(src, dst, send, recv, where):
        return pltpu.make_async_remote_copy(
            src_ref=src, dst_ref=dst, send_sem=send, recv_sem=recv, device_id=where,
            device_id_type=MESH,
        )

    loads = []

    def load(src, dst, index):
        copy = pltpu.make_async_copy(src, dst, in_sem.at[index])
        copy.start()
        return copy

    load_q = load(q_hbm, q_ref, 0)
    load_sk = load(sk_hbm, sk_ref, 1)
    load_sv = load(sv_hbm, sv_ref, 2)
    load_k = [
        load(k_hbm.at[pl.ds(j * KEY_BLOCK, KEY_BLOCK)], k_ref.at[pl.ds(j * KEY_BLOCK, KEY_BLOCK)], 3 + j)
        for j in range(BLOCKS)
    ]
    load_v = load(v_hbm, v_ref, 3 + BLOCKS)

    def w_slot(hh, xx):
        return wg.at[hh, pl.ds(pl.multiple_of(xx * WCOLS, WCOLS), WCOLS)]

    z_partner = device(pool, x, y, 1 - h, t)
    x_partners = [lax.rem(x + k, 4) for k in (1, 3, 2)]
    own_w = pltpu.make_async_copy(w_hbm, w_slot(h, x), w_loc)
    own_w.start()
    w_over = remote(w_hbm, w_slot(h, x), w_zs, w_rs.at[h, x], z_partner)
    w_over.start()
    w_first = [
        remote(w_hbm, w_slot(h, x), w_xs.at[0, i], w_rs.at[h, x], device(pool, xx, y, h, t))
        for i, xx in enumerate(x_partners)
    ]
    for copy in w_first:
        copy.start()

    def w_arrival(hh, xx):
        return remote(w_slot(hh, xx), w_slot(hh, xx), w_zs, w_rs.at[hh, xx], z_partner)

    def res_plan(s):
        to_y = jnp.where(zero_pool, ylo * 2 + h, s)
        to_h = jnp.where(zero_pool, s % 2, h)
        slot = jnp.where(zero_pool, yhi * 2 + s // 2, y)
        keeps = jnp.logical_and(to_y == y, to_h == h)
        return keeps, slot, device(pool, x, to_y, to_h, t)

    def res_copies(s):
        keeps, slot, where = res_plan(s)
        near = pltpu.make_async_copy(res_hbm.at[s], rres.at[slot], res_rs.at[slot])
        far = remote(res_hbm.at[s], rres.at[slot], res_ss.at[s], res_rs.at[slot], where)
        return keeps, near, far

    for s in range(4):
        keeps, near, far = res_copies(s)

        @pl.when(keeps)
        def _():
            near.start()

        @pl.when(jnp.logical_not(keeps))
        def _():
            far.start()

    plen = plen_ref[0, 0]
    slen = slen_ref[0, 0]
    row_at = lax.broadcasted_iota(jnp.int32, (SPAN, SPAN), 0)
    col_at = lax.broadcasted_iota(jnp.int32, (SPAN, SPAN), 1)
    span_mask = (col_at <= row_at) & (col_at < slen)

    def head_rows(g):
        return slice(g * SPAN, (g + 1) * SPAN)

    def head_cols(hd, g):
        return slice((hd * GROUP_HEADS + g) * HD, (hd * GROUP_HEADS + g + 1) * HD)

    def span_scores(hd):
        for g in range(GROUP_HEADS):
            s = nt(qs[hd, head_rows(g), :], sk_ref[:, hd * HD : (hd + 1) * HD])
            s = jnp.where(span_mask, s, MASKED)
            Sp[hd, head_rows(g), :] = s
            rest = s[:, HD:]
            mx[hd, head_rows(g), :] = jnp.maximum(
                s[:, :HD], jnp.concatenate([rest, rest], axis=1)
            )

    def scores(hd, j):
        base = pl.multiple_of(j * KEY_BLOCK, KEY_BLOCK)
        keys = k_ref[pl.ds(base, KEY_BLOCK), hd * HD : (hd + 1) * HD]
        position = base + lax.broadcasted_iota(jnp.int32, (1, KEY_BLOCK), 1)
        bias = jnp.where(position < plen, 0.0, MASKED)
        slot = lax.rem(hd * BLOCKS + j, 3)
        for g in range(GROUP_HEADS):
            s = nt(qs[hd, head_rows(g), :], keys) + bias
            S[slot, head_rows(g), :] = s
            m = mx[hd, head_rows(g), :]
            for u in range(0, KEY_BLOCK, HD):
                m = jnp.maximum(m, s[:, u : u + HD])
            mx[hd, head_rows(g), :] = m

    def finish_max(hd):
        m = jnp.max(mx[hd], axis=1, keepdims=True) * LOG2
        mx[hd] = jnp.broadcast_to(m, (ROWS, HD))

    def weigh(hd, j):
        base = pl.multiple_of(j * KEY_BLOCK, KEY_BLOCK)
        values = va[hd, pl.ds(base, KEY_BLOCK), :]
        slot = lax.rem(hd * BLOCKS + j, 3)
        for g in range(GROUP_HEADS):
            m = mx[hd, head_rows(g), :]
            wide = jnp.concatenate([m] * (KEY_BLOCK // HD), axis=1)
            p = jnp.exp2(S[slot, head_rows(g), :] * LOG2 - wide).astype(jnp.bfloat16)
            acc[hd, head_rows(g), :] += jnp.dot(p, values, preferred_element_type=jnp.float32)

    def span_weigh(hd):
        for g in range(GROUP_HEADS):
            m = mx[hd, head_rows(g), :]
            wide = jnp.concatenate([m, m[:, : SPAN - HD]], axis=1)
            p = jnp.exp2(Sp[hd, head_rows(g), :] * LOG2 - wide).astype(jnp.bfloat16)
            acc[hd, head_rows(g), :] = jnp.dot(p, vas[hd], preferred_element_type=jnp.float32)

    def a_slot(hd, yy):
        return ag.at[hd, pl.ds(pl.multiple_of(yy * SPAN, SPAN), SPAN)]

    def attended(hd):
        for g in range(GROUP_HEADS):
            a = acc[hd, head_rows(g), :]
            out = (a[:, :HD] / a[:, HD:]).astype(jnp.bfloat16)
            ag[hd, pl.ds(pl.multiple_of(y * SPAN, SPAN), SPAN), g * HD : (g + 1) * HD] = out

    y_partners = [yhi * 2 + 1 - ylo, (1 - yhi) * 2 + ylo, (1 - yhi) * 2 + 1 - ylo]

    def a_copies(hd):
        return [
            remote(a_slot(hd, y), a_slot(hd, y), a_ss.at[hd, i], a_rs.at[hd, y], device(pool, x, yy, h, t))
            for i, yy in enumerate(y_partners)
        ]

    def a_arrival(hd, yy):
        return remote(a_slot(hd, yy), a_slot(hd, yy), a_ss.at[hd, 0], a_rs.at[hd, yy], z_partner)

    load_q.wait()
    for hd in range(KVL):
        for g in range(GROUP_HEADS):
            qs[hd, head_rows(g), :] = q_ref[:, head_cols(hd, g)]
    load_sk.wait()
    span_scores(0)
    for copy in load_k:
        copy.wait()
    pl.loop(0, BLOCKS)(lambda j: scores(0, j))
    load_v.wait()
    load_sv.wait()
    for hd in range(KVL):
        va[hd, :, :HD] = v_ref[:, hd * HD : (hd + 1) * HD]
        va[hd, :, HD:] = jnp.ones((PREFIX, HD), jnp.bfloat16)
        vas[hd, :, :HD] = sv_ref[:, hd * HD : (hd + 1) * HD]
        vas[hd, :, HD:] = jnp.ones((SPAN, HD), jnp.bfloat16)
    finish_max(0)
    span_weigh(0)
    span_scores(1)

    def middle(j):
        weigh(0, j)
        scores(1, j)

    pl.loop(0, BLOCKS)(middle)
    attended(0)
    first_a = a_copies(0)
    for copy in first_a:
        copy.start()
    finish_max(1)
    span_weigh(1)
    pl.loop(0, BLOCKS)(lambda j: weigh(1, j))
    attended(1)
    second_a = a_copies(1)
    for copy in second_a:
        copy.start()

    w_arrival(1 - h, x).wait_recv()
    w_second = [
        remote(
            w_slot(1 - h, x), w_slot(1 - h, x), w_xs.at[1, i], w_rs.at[1 - h, x], device(pool, xx, y, h, t)
        )
        for i, xx in enumerate(x_partners)
    ]
    for copy in w_second:
        copy.start()

    t1 = t + 1 - 2 * lax.rem(t, 2)
    t2 = lax.rem(t + 2, 4)
    t3 = 3 - t
    tpar = lax.rem(t, 2)
    thi = lax.div(t, 2)

    def piece_rows(piece):
        return pl.ds(pl.multiple_of(piece * WCOLS, WCOLS), WCOLS)

    def p1_copy(u, i, piece):
        return remote(
            pb.at[u, piece_rows(piece)], rcv1.at[lax.div(piece, 2), u], p1_ss.at[u, i],
            p1_rs.at[lax.div(piece, 2), u], device(pool, x, y, h, t1),
        )

    def p1_arrival(jj, u):
        return remote(rcv1.at[jj, u], rcv1.at[jj, u], p1_ss.at[u, 0], p1_rs.at[jj, u], z_partner)

    def p2_copy(u):
        return remote(s2.at[u], rcv2.at[u], p2_ss.at[u], p2_rs.at[u], device(pool, x, y, h, t2))

    def unit(u):
        hh = h if u < 2 else 1 - h
        pair = yhi if u % 2 == 0 else 1 - yhi
        rows = pl.ds(pl.multiple_of(pair * 2 * SPAN, 2 * SPAN), 2 * SPAN)
        total = nt(wg[hh, :, :HALF], ag[0, rows, :]) + nt(wg[hh, :, HALF:], ag[1, rows, :])
        pr[u] = total
        pb[u] = total.astype(jnp.bfloat16)
        sent = [p1_copy(u, 0, t3), p1_copy(u, 1, t1)]
        for copy in sent:
            copy.start()
        return sent

    def second(u):
        p1_arrival(1 - thi, u).wait_recv()
        total = pr[u, piece_rows(t2), :] + rcv1[1 - thi, u].astype(jnp.float32)
        s2[u] = total.astype(jnp.bfloat16)
        copy = p2_copy(u)
        copy.start()
        return copy

    p1_sent = []
    p2_sent = []
    own_w.wait()
    for xx in x_partners:
        w_arrival(h, xx).wait_recv()
    for hd in range(KVL):
        a_arrival(hd, y_partners[0]).wait_recv()
    p1_sent += unit(0)
    for hd in range(KVL):
        for yy in y_partners[1:]:
            a_arrival(hd, yy).wait_recv()
    p1_sent += unit(1)
    p2_sent.append(second(0))
    for xx in x_partners:
        w_arrival(1 - h, xx).wait_recv()
    p1_sent += unit(2)
    p2_sent.append(second(1))
    p1_sent += unit(3)
    p2_sent.append(second(2))
    p2_sent.append(second(3))

    def final_copy(s, slot_from, index):
        to_y = jnp.where(zero_pool, s, lax.div(s, 2) * 2 + yhi)
        to_h = jnp.where(zero_pool, h, ylo)
        slot = jnp.where(zero_pool, y, lax.rem(s, 2) * 2 + h)
        return remote(
            lb.at[slot_from], st.at[slot], f_ss.at[index], f_rs.at[slot],
            device(1 - pool, x, to_y, to_h, t),
        )

    turn[pl.ds(PIECE, 64), :] = jnp.zeros((64, 2 * SPAN), jnp.float32)
    final_sent = []
    for pp in range(2):
        pair = yhi if pp == 0 else 1 - yhi
        for hh in range(2):
            u = hh * 2 + pp
            at = h if hh == 0 else 1 - h
            p1_arrival(thi, u).wait_recv()
            p2_copy(u).wait_recv()
            total = (
                pr[u, piece_rows(t), :]
                + rcv1[thi, u].astype(jnp.float32)
                + rcv2[u].astype(jnp.float32)
            )
            turn[pl.ds(pl.multiple_of(at * WCOLS, WCOLS), WCOLS), :] = total
        whole = jnp.transpose(turn[...])[:, :PIECE]
        for a in range(2):
            s = pair * 2 + a
            pltpu.make_async_copy(rres.at[s], rres.at[s], res_rs.at[s]).wait()
            out = whole[a * SPAN : (a + 1) * SPAN] + rres[s].astype(jnp.float32)
            lb[pp * 2 + a] = out.astype(jnp.bfloat16)
            copy = final_copy(s, pp * 2 + a, pp * 2 + a)
            copy.start()
            final_sent.append(copy)

    own_index = (ylo * 2 + h) * 4 + t
    ones = jnp.ones((8, PIECE), jnp.float32)
    row_sums = []
    for s in range(4):
        remote(lb.at[s], st.at[s], f_ss.at[s], f_rs.at[s], z_partner).wait_recv()
        tile = st[s].astype(jnp.float32)
        row_sums.append(nt(ones, tile * tile, lax.Precision.HIGHEST))
    stream_out = pltpu.make_async_copy(st, stream_hbm, out_sem.at[0])
    stream_out.start()
    across = row_sums[0] + row_sums[1] + row_sums[2] + row_sums[3]
    sub = lax.broadcasted_iota(jnp.int32, (8, SPAN), 0)
    mine = jnp.zeros((8, SPAN), jnp.float32)
    for s in range(4):
        mine = jnp.where(sub == s, row_sums[s], mine)
    mine = jnp.where(zero_pool, mine, across)
    sums[own_index, :, :SPAN] = mine
    sums[own_index, :, SPAN:] = jnp.zeros((8, 256 - SPAN), jnp.float32)
    sum_sent = []
    for k in range(1, 16):
        to_y = yhi * 2 + lax.rem(ylo + k // 8, 2)
        to_h = lax.rem(h + (k // 4) % 2, 2)
        to_t = lax.rem(t + k % 4, 4)
        copy = remote(
            sums.at[own_index], sums.at[own_index], q_ss.at[k], q_rs.at[own_index],
            device(pool, x, to_y, to_h, to_t),
        )
        copy.start()
        sum_sent.append(copy)
    total = mine
    for k in range(1, 16):
        from_y = lax.rem(ylo + k // 8, 2)
        from_h = lax.rem(h + (k // 4) % 2, 2)
        index = (from_y * 2 + from_h) * 4 + lax.rem(t + k % 4, 4)
        remote(sums.at[index], sums.at[index], q_ss.at[k], q_rs.at[index], z_partner).wait_recv()
        part = sums[index, :, :SPAN]
        if k >= 4:
            part = jnp.where(zero_pool, part, 0.0)
        total = total + part
    scale = lax.rsqrt(total * (1.0 / D) + EPSILON)
    for s in range(4):
        picked = jnp.where(sub == s, scale, 0.0)
        wide = lax.dot_general(
            picked, ones, (((0,), (0,)), ((), ())), preferred_element_type=jnp.float32,
            precision=lax.Precision.HIGHEST,
        )
        gain_at = jnp.where(zero_pool, ylo * 2 + h, s)
        gain = gain_ref[pl.ds(gain_at, 1), :]
        nm[s] = (st[s].astype(jnp.float32) * wide * gain).astype(jnp.bfloat16)
    normed_out = pltpu.make_async_copy(nm, normed_hbm, out_sem.at[1])
    normed_out.start()

    w_over.wait_send()
    for copy in w_first + w_second + first_a + second_a + p1_sent + p2_sent + final_sent + sum_sent:
        copy.wait_send()
    for s in range(4):
        keeps, near, far = res_copies(s)

        @pl.when(jnp.logical_not(keeps))
        def _():
            far.wait_send()

    stream_out.wait()
    normed_out.wait()


def fused(plen, slen, q, k, v, sk, sv, w, res, gain):
    smem = pl.BlockSpec(memory_space=pltpu.SMEM)
    vmem = pl.BlockSpec(memory_space=pltpu.VMEM)
    hbm = pl.BlockSpec(memory_space=pl.ANY)
    dma = pltpu.SemaphoreType.DMA
    bf, f32 = jnp.bfloat16, jnp.float32
    out = jax.ShapeDtypeStruct((4, SPAN, PIECE), bf)
    return pl.pallas_call(
        body,
        out_shape=(out, out),
        in_specs=[smem, smem] + [hbm] * 7 + [vmem],
        out_specs=(hbm, hbm),
        scratch_shapes=[
            pltpu.VMEM((SPAN, 2 * HALF), bf),
            pltpu.VMEM((PREFIX, KVL * HD), bf),
            pltpu.VMEM((PREFIX, KVL * HD), bf),
            pltpu.VMEM((SPAN, KVL * HD), bf),
            pltpu.VMEM((SPAN, KVL * HD), bf),
            pltpu.VMEM((KVL, ROWS, HD), bf),
            pltpu.VMEM((3, ROWS, KEY_BLOCK), f32),
            pltpu.VMEM((KVL, ROWS, SPAN), f32),
            pltpu.VMEM((KVL, ROWS, HD), f32),
            pltpu.VMEM((KVL, ROWS, 2 * HD), f32),
            pltpu.VMEM((KVL, PREFIX, 2 * HD), bf),
            pltpu.VMEM((KVL, SPAN, 2 * HD), bf),
            pltpu.VMEM((2, 4 * WCOLS, 2 * HALF), bf),
            pltpu.VMEM((KVL, 4 * SPAN, HALF), bf),
            pltpu.VMEM((4, 4 * WCOLS, 2 * SPAN), f32),
            pltpu.VMEM((4, 4 * WCOLS, 2 * SPAN), bf),
            pltpu.VMEM((2, 4, WCOLS, 2 * SPAN), bf),
            pltpu.VMEM((4, WCOLS, 2 * SPAN), bf),
            pltpu.VMEM((4, WCOLS, 2 * SPAN), bf),
            pltpu.VMEM((4, SPAN, PIECE), bf),
            pltpu.VMEM((PIECE + 64, 2 * SPAN), f32),
            pltpu.VMEM((4, SPAN, PIECE), bf),
            pltpu.VMEM((4, SPAN, PIECE), bf),
            pltpu.VMEM((4, SPAN, PIECE), bf),
            pltpu.VMEM((16, 8, 256), f32),
            dma((4 + BLOCKS,)),
            dma,
            dma,
            dma((2, 3)),
            dma((2, 4)),
            dma((KVL, 3)),
            dma((KVL, 4)),
            dma((4,)),
            dma((4,)),
            dma((4, 2)),
            dma((2, 4)),
            dma((4,)),
            dma((4,)),
            dma((4,)),
            dma((4,)),
            dma((16,)),
            dma((16,)),
            dma((2,)),
        ],
        compiler_params=pltpu.CompilerParams(has_side_effects=True, vmem_limit_bytes=60 << 20),
        name="fused",
    )(plen, slen, q, k, v, sk, sv, w, res, gain)


def shards(
    queries, new_keys, new_values, cache_keys, cache_values, prefix_len, span_len, residual, out_proj,
    norm_gain,
):
    zero_pool = lax.axis_index("pool") == 0
    own = residual[0]
    pieces = jnp.where(
        zero_pool,
        own.reshape(4, SPAN, PIECE),
        jnp.transpose(own.reshape(SPAN, 4, PIECE), (1, 0, 2)),
    )
    stream, normed = fused(
        prefix_len, span_len, queries[0], cache_keys[0, 0], cache_values[0, 0], new_keys[0],
        new_values[0], jnp.swapaxes(out_proj[0], 0, 1), pieces, norm_gain[0].reshape(4, PIECE),
    )

    def whole(four):
        return jnp.where(
            zero_pool,
            four.reshape(SPAN, 4 * PIECE),
            jnp.transpose(four, (1, 0, 2)).reshape(SPAN, 4 * PIECE),
        )

    return whole(stream)[None], whole(normed)[None]


def solution(mesh):
    placed = (
        P("pool", "group", "tensor"),
        P("pool", "group", "tensor"),
        P("pool", "group", "tensor"),
        P("pool", "group", None, "tensor"),
        P("pool", "group", None, "tensor"),
        P("pool", "group"),
        P("pool", "group"),
        P("pool", "group", "tensor"),
        P("pool", "tensor", "group"),
        P("pool", "tensor"),
    )
    return jax.shard_map(
        shards,
        mesh=mesh,
        in_specs=placed,
        out_specs=(P("pool", "group", "tensor"), P("pool", "group", "tensor")),
        check_vma=False,
    )
```

```python
import functools
import math

import jax
import jax.numpy as jnp
from jax import lax
from jax.experimental import pallas as pl
from jax.experimental.pallas import tpu as pltpu
from jax.sharding import PartitionSpec as P

D = 5120
HD = 128
KVL = 2
GROUP_HEADS = 5
PREFIX = 4096
SPAN = 192
ROWS = GROUP_HEADS * SPAN
HALF = GROUP_HEADS * HD
EPSILON = 1e-6
KEY_BLOCK = 2048
BLOCKS = PREFIX // KEY_BLOCK
PIECE = 320
WCOLS = 160
WHALF = 80
LOG2 = math.log2(math.e) / math.sqrt(HD)
MASKED = -1e30
MESH = pl.DeviceIdType.MESH


def nt(a, b, precision=None):
    return lax.dot_general(
        a, b, (((1,), (1,)), ((), ())), preferred_element_type=jnp.float32, precision=precision
    )


def body(
    plen_ref, slen_ref, q_hbm, k_hbm, v_hbm, sk_hbm, sv_hbm, res_hbm, w_hbm, gain_ref,
    stream_hbm, normed_hbm,
    q_ref, k_ref, v_ref, sk_ref, sv_ref, res_ref, p32, rp, tiles,
    qs, S, Sp, mx, acc, va, vas,
    wg, ag, pr, pb, rcv1, s2, rcv2, rres, rt, turn, lb, st, sums, mean, means,
    in_sem, w_loc, w_zs, w_xs, w_rs, a_ss, a_rs, res_ss, res_rs,
    p1_ss, p1_rs, p2_ss, p2_rs, f_ss, f_rs, q_ss, q_rs, m_ss, m_rs, out_sem,
):
    pool = lax.axis_index("pool")
    group = lax.axis_index("group")
    t = lax.axis_index("tensor")
    h = lax.rem(group, 2)
    y = lax.rem(lax.div(group, 2), 4)
    x = lax.div(group, 8)
    ylo = lax.rem(y, 2)
    yhi = lax.div(y, 2)
    zero_pool = pool == 0

    def device(px, xx, yy, hh, tt):
        return (px, (xx * 4 + yy) * 2 + hh, tt)

    def remote(src, dst, send, recv, where):
        return pltpu.make_async_remote_copy(
            src_ref=src, dst_ref=dst, send_sem=send, recv_sem=recv, device_id=where,
            device_id_type=MESH,
        )

    barrier = pltpu.get_barrier_semaphore()
    peers = [
        (lax.rem(y + k // 4, 4), lax.rem(t + k % 4, 4)) for k in range(1, 16)
    ]
    friends = [device(pool, x, yy, h, tt) for yy, tt in peers]
    friends += [device(pool, x, a, 1 - h, t) for a in range(4)]
    friends += [device(pool, lax.rem(x + k, 4), y, h, t) for k in (1, 2, 3)]
    friends += [device(1 - pool, x, a, b, t) for a in range(4) for b in range(2)]
    for friend in friends:
        pl.semaphore_signal(barrier, 1, device_id=friend, device_id_type=MESH)

    def put(s, rows, value):
        blank = jnp.zeros((value.shape[0], 3 * HD - PIECE), jnp.float32)
        full = jnp.concatenate([value, blank], axis=1)
        for c in range(3):
            p32[s, c, rows, :] = full[:, c * HD : (c + 1) * HD]

    def get(s, rows):
        full = jnp.concatenate([p32[s, c, rows, :] for c in range(3)], axis=1)
        return full[:, :PIECE]

    every = slice(0, SPAN)

    def every_fourth(k):
        return pl.ds(k, SPAN // 4, stride=4)


    def load(src, dst, index):
        copy = pltpu.make_async_copy(src, dst, in_sem.at[index])
        copy.start()
        return copy

    load_q = load(q_hbm, q_ref, 0)
    load_sk = load(sk_hbm, sk_ref, 1)
    load_sv = load(sv_hbm, sv_ref, 2)
    load_k = [
        load(k_hbm.at[pl.ds(j * KEY_BLOCK, KEY_BLOCK)], k_ref.at[pl.ds(j * KEY_BLOCK, KEY_BLOCK)], 3 + j)
        for j in range(BLOCKS)
    ]
    load_v = load(v_hbm, v_ref, 3 + BLOCKS)
    load_res = load(res_hbm, res_ref, 4 + BLOCKS)

    sums[y * 4 + t] = jnp.zeros((8, 2 * SPAN), jnp.float32)

    def w_half(hh, xx, part):
        return wg.at[hh, pl.ds(pl.multiple_of(xx * WCOLS + part * WHALF, 16), WHALF)]

    def w_from(part):
        return w_hbm.at[pl.ds(part * WHALF, WHALF)]

    z_partner = device(pool, x, y, 1 - h, t)
    x_up, x_down, x_far = lax.rem(x + 1, 4), lax.rem(x + 3, 4), lax.rem(x + 2, 4)
    own_w = pltpu.make_async_copy(
        w_hbm, wg.at[h, pl.ds(pl.multiple_of(x * WCOLS, WCOLS), WCOLS)], w_loc
    )
    own_w.start()
    w_over = [
        remote(w_from(part), w_half(h, x, part), w_zs.at[part], w_rs.at[h, x, part], z_partner)
        for part in range(2)
    ]

    def w_send(source, hh, xx, part, wave, way, to_x):
        return remote(
            source, w_half(hh, xx, part), w_xs.at[wave, part, way], w_rs.at[hh, xx, part],
            device(pool, to_x, y, h, t),
        )

    def w_direct(wave):
        hh = h if wave == 0 else 1 - h
        out = []
        for part in range(2):
            source = w_from(part) if wave == 0 else w_half(hh, x, part)
            ways = [(0, x_up), (1, x_down)]
            for way, to_x in ways if part == 0 else ways[::-1]:
                out.append(w_send(source, hh, x, part, wave, way, to_x))
        return out

    def w_onward(wave):
        hh = h if wave == 0 else 1 - h
        return [
            w_send(w_half(hh, x_down, 0), hh, x_down, 0, wave, 2, x_up),
            w_send(w_half(hh, x_up, 1), hh, x_up, 1, wave, 2, x_down),
        ]

    def w_wait(hh, xx, part):
        remote(
            w_half(hh, xx, part), w_half(hh, xx, part), w_zs.at[0], w_rs.at[hh, xx, part], z_partner
        ).wait_recv()

    def pass_on(wave):
        hh = h if wave == 0 else 1 - h
        copies = w_onward(wave)
        w_wait(hh, x_down, 0)
        copies[0].start()
        w_wait(hh, x_up, 1)
        copies[1].start()
        return copies

    def w_rest(hh):
        w_wait(hh, x_down, 1)
        w_wait(hh, x_up, 0)
        w_wait(hh, x_far, 0)
        w_wait(hh, x_far, 1)

    def res_plan(s):
        to_y = jnp.where(zero_pool, ylo * 2 + h, s)
        to_h = jnp.where(zero_pool, s % 2, h)
        slot = jnp.where(zero_pool, yhi * 2 + s // 2, y)
        keeps = jnp.logical_and(to_y == y, to_h == h)
        return keeps, slot, device(pool, x, to_y, to_h, t)

    def res_copies(s):
        keeps, slot, where = res_plan(s)
        near = pltpu.make_async_copy(rp.at[s], rres.at[slot], res_rs.at[slot])
        far = remote(rp.at[s], rres.at[slot], res_ss.at[s], res_rs.at[slot], where)
        return keeps, near, far

    plen = plen_ref[0, 0]
    slen = slen_ref[0, 0]
    row_at = lax.broadcasted_iota(jnp.int32, (SPAN, SPAN), 0)
    col_at = lax.broadcasted_iota(jnp.int32, (SPAN, SPAN), 1)
    span_mask = (col_at <= row_at) & (col_at < slen)

    def head_rows(g):
        return slice(g * SPAN, (g + 1) * SPAN)

    def head_cols(hd, g):
        return slice((hd * GROUP_HEADS + g) * HD, (hd * GROUP_HEADS + g + 1) * HD)

    def span_scores(hd):
        for g in range(GROUP_HEADS):
            s = nt(qs[hd, head_rows(g), :], sk_ref[:, hd * HD : (hd + 1) * HD])
            s = jnp.where(span_mask, s, MASKED)
            Sp[hd, head_rows(g), :] = s
            rest = s[:, HD:]
            mx[hd, head_rows(g), :] = jnp.maximum(
                s[:, :HD], jnp.concatenate([rest, rest], axis=1)
            )

    def scores(hd, j):
        base = pl.multiple_of(j * KEY_BLOCK, KEY_BLOCK)
        keys = k_ref[pl.ds(base, KEY_BLOCK), hd * HD : (hd + 1) * HD]
        position = base + lax.broadcasted_iota(jnp.int32, (1, KEY_BLOCK), 1)
        bias = jnp.where(position < plen, 0.0, MASKED)
        slot = lax.rem(hd * BLOCKS + j, 3)
        for g in range(GROUP_HEADS):
            s = nt(qs[hd, head_rows(g), :], keys) + bias
            S[slot, head_rows(g), :] = s
            m = mx[hd, head_rows(g), :]
            for u in range(0, KEY_BLOCK, HD):
                m = jnp.maximum(m, s[:, u : u + HD])
            mx[hd, head_rows(g), :] = m

    def finish_max(hd):
        m = jnp.max(mx[hd], axis=1, keepdims=True) * LOG2
        mx[hd] = jnp.broadcast_to(m, (ROWS, HD))

    def weigh(hd, j):
        base = pl.multiple_of(j * KEY_BLOCK, KEY_BLOCK)
        values = va[hd, pl.ds(base, KEY_BLOCK), :]
        slot = lax.rem(hd * BLOCKS + j, 3)
        for g in range(GROUP_HEADS):
            m = mx[hd, head_rows(g), :]
            wide = jnp.concatenate([m] * (KEY_BLOCK // HD), axis=1)
            p = jnp.exp2(S[slot, head_rows(g), :] * LOG2 - wide).astype(jnp.bfloat16)
            acc[hd, head_rows(g), :] += jnp.dot(p, values, preferred_element_type=jnp.float32)

    def span_weigh(hd):
        for g in range(GROUP_HEADS):
            m = mx[hd, head_rows(g), :]
            wide = jnp.concatenate([m, m[:, : SPAN - HD]], axis=1)
            p = jnp.exp2(Sp[hd, head_rows(g), :] * LOG2 - wide).astype(jnp.bfloat16)
            acc[hd, head_rows(g), :] = jnp.dot(p, vas[hd], preferred_element_type=jnp.float32)

    def a_slot(hd, yy):
        return ag.at[hd, pl.ds(pl.multiple_of(yy * SPAN, SPAN), SPAN)]

    def attended(hd):
        for g in range(GROUP_HEADS):
            a = acc[hd, head_rows(g), :]
            out = (a[:, :HD] / a[:, HD:]).astype(jnp.bfloat16)
            ag[hd, pl.ds(pl.multiple_of(y * SPAN, SPAN), SPAN), g * HD : (g + 1) * HD] = out

    y_partners = [yhi * 2 + 1 - ylo, (1 - yhi) * 2 + ylo, (1 - yhi) * 2 + 1 - ylo]

    y_up, y_down = lax.rem(y + 1, 4), lax.rem(y + 3, 4)

    def a_copy(hd, yy, i, to_y):
        return remote(a_slot(hd, yy), a_slot(hd, yy), a_ss.at[hd, i], a_rs.at[hd, yy], device(pool, x, to_y, h, t))

    def a_copies(hd):
        return [a_copy(hd, y, 0, y_up), a_copy(hd, y, 1, y_down)]

    def a_arrival(hd, yy):
        return remote(a_slot(hd, yy), a_slot(hd, yy), a_ss.at[hd, 0], a_rs.at[hd, yy], z_partner)

    pl.semaphore_wait(barrier, len(friends))
    w_first = w_direct(0)
    for copy in w_over + w_first:
        copy.start()
    load_q.wait()
    for hd in range(KVL):
        for g in range(GROUP_HEADS):
            qs[hd, head_rows(g), :] = q_ref[:, head_cols(hd, g)]
    load_sk.wait()
    span_scores(0)
    for copy in load_k:
        copy.wait()
    pl.loop(0, BLOCKS)(lambda j: scores(0, j))
    load_v.wait()
    load_sv.wait()
    for hd in range(KVL):
        va[hd, :, :HD] = v_ref[:, hd * HD : (hd + 1) * HD]
        va[hd, :, HD:] = jnp.ones((PREFIX, HD), jnp.bfloat16)
        vas[hd, :, :HD] = sv_ref[:, hd * HD : (hd + 1) * HD]
        vas[hd, :, HD:] = jnp.ones((SPAN, HD), jnp.bfloat16)
    finish_max(0)
    span_weigh(0)
    span_scores(1)

    def middle(j):
        weigh(0, j)
        scores(1, j)

    pl.loop(0, BLOCKS)(middle)
    attended(0)
    first_a = a_copies(0)
    for copy in first_a:
        copy.start()
    w_first += pass_on(0)
    finish_max(1)
    span_weigh(1)
    pl.loop(0, BLOCKS)(lambda j: weigh(1, j))
    attended(1)
    second_a = a_copies(1)
    for copy in second_a:
        copy.start()

    a_arrival(0, y_down).wait_recv()
    pass_first = a_copy(0, y_down, 2, y_up)
    pass_first.start()
    load_res.wait()

    @pl.when(zero_pool)
    def _():
        for s in range(4):
            rows = res_ref[s * (SPAN // 4) : (s + 1) * (SPAN // 4), :].astype(jnp.float32)
            for k in range(4):
                put(s, every_fourth(k), rows[:, k * PIECE : (k + 1) * PIECE])

    @pl.when(jnp.logical_not(zero_pool))
    def _():
        for s in range(4):
            put(s, every, res_ref[:, s * PIECE : (s + 1) * PIECE].astype(jnp.float32))

    for s in range(4):
        rp[s] = get(s, every).astype(jnp.bfloat16)
        keeps, near, far = res_copies(s)

        @pl.when(keeps)
        def _():
            near.start()

        @pl.when(jnp.logical_not(keeps))
        def _():
            far.start()

    w_second = w_direct(1)
    for part in range(2):
        w_wait(1 - h, x, part)
        for copy in w_second[2 * part : 2 * part + 2]:
            copy.start()
    a_arrival(1, y_up).wait_recv()
    pass_second = a_copy(1, y_up, 2, y_down)
    pass_second.start()

    t1 = t + 1 - 2 * lax.rem(t, 2)
    t2 = lax.rem(t + 2, 4)
    t3 = 3 - t
    tpar = lax.rem(t, 2)
    thi = lax.div(t, 2)

    def piece_rows(piece):
        return pl.ds(pl.multiple_of(piece * WCOLS, WCOLS), WCOLS)

    def p1_copy(u, i, piece):
        return remote(
            pb.at[u, piece_rows(piece)], rcv1.at[lax.div(piece, 2), u], p1_ss.at[u, i],
            p1_rs.at[lax.div(piece, 2), u], device(pool, x, y, h, t1),
        )

    def p1_arrival(jj, u):
        return remote(rcv1.at[jj, u], rcv1.at[jj, u], p1_ss.at[u, 0], p1_rs.at[jj, u], z_partner)

    def p2_copy(u):
        return remote(s2.at[u], rcv2.at[u], p2_ss.at[u], p2_rs.at[u], device(pool, x, y, h, t2))

    def unit(u):
        hh = h if u < 2 else 1 - h
        pair = yhi if u % 2 == 0 else 1 - yhi
        rows = pl.ds(pl.multiple_of(pair * 2 * SPAN, 2 * SPAN), 2 * SPAN)
        total = nt(wg[hh, :, :HALF], ag[0, rows, :]) + nt(wg[hh, :, HALF:], ag[1, rows, :])
        pr[u] = total
        pb[u] = total.astype(jnp.bfloat16)
        sent = [p1_copy(u, 0, t3), p1_copy(u, 1, t1)]
        for copy in sent:
            copy.start()
        return sent

    def second(u):
        p1_arrival(1 - thi, u).wait_recv()
        total = pr[u, piece_rows(t2), :] + rcv1[1 - thi, u].astype(jnp.float32)
        s2[u] = total.astype(jnp.bfloat16)
        copy = p2_copy(u)
        copy.start()
        return copy

    p1_sent = []
    p2_sent = []
    own_w.wait()
    w_rest(h)
    first_head = jnp.where(ylo == 0, 0, 1)
    a_arrival(first_head, y_partners[0]).wait_recv()
    p1_sent += unit(0)
    a_arrival(1 - first_head, y_partners[2]).wait_recv()
    for hd in range(KVL):
        a_arrival(hd, y_partners[1]).wait_recv()
    p1_sent += unit(1)
    w_second += pass_on(1)
    p2_sent.append(second(0))
    p2_sent.append(second(1))

    for pair in range(2):
        for a in range(2):
            at = pair * 2 + a
            pltpu.make_async_copy(rres.at[at], rres.at[at], res_rs.at[at]).wait()
        both = jnp.concatenate([rres[pair * 2], rres[pair * 2 + 1]], axis=0).astype(jnp.float32)
        blank = jnp.zeros((2 * SPAN, 3 * HD - PIECE), jnp.float32)
        rt[pair] = jnp.transpose(jnp.concatenate([both, blank], axis=1))

    w_rest(1 - h)
    p1_sent += unit(2)
    p1_sent += unit(3)
    p2_sent.append(second(2))
    p2_sent.append(second(3))

    def final_copy(s, slot_from, index):
        to_y = jnp.where(zero_pool, s, lax.div(s, 2) * 2 + yhi)
        to_h = jnp.where(zero_pool, h, ylo)
        slot = jnp.where(zero_pool, y, lax.rem(s, 2) * 2 + h)
        return remote(
            lb.at[slot_from], st.at[slot], f_ss.at[index], f_rs.at[slot],
            device(1 - pool, x, to_y, to_h, t),
        )

    turn[pl.ds(PIECE, 64), :] = jnp.zeros((64, 2 * SPAN), jnp.float32)
    own_index = y * 4 + t
    final_sent = []
    sum_sent = []
    for pp in range(2):
        pair = yhi if pp == 0 else 1 - yhi
        squares = jnp.zeros((1, 2 * SPAN), jnp.float32)
        for hh in range(2):
            u = hh * 2 + pp
            at = h if hh == 0 else 1 - h
            p1_arrival(thi, u).wait_recv()
            p2_copy(u).wait_recv()
            rows = pl.ds(pl.multiple_of(at * WCOLS, WCOLS), WCOLS)
            total = (
                pr[u, piece_rows(t), :]
                + rcv1[thi, u].astype(jnp.float32)
                + rcv2[u].astype(jnp.float32)
                + rt[pair, rows, :]
            )
            total = total.astype(jnp.bfloat16).astype(jnp.float32)
            turn[rows, :] = total
            squares = squares + jnp.sum(total * total, axis=0, keepdims=True)
        sums[own_index, pl.ds(pair, 1), :] = squares
        if pp == 1:
            for k, (yy, tt) in enumerate(peers):
                copy = remote(
                    sums.at[own_index], sums.at[own_index], q_ss.at[k], q_rs.at[own_index],
                    device(pool, x, yy, h, tt),
                )
                copy.start()
                sum_sent.append(copy)
        whole = jnp.transpose(turn[...])[:, :PIECE].astype(jnp.bfloat16)
        for a in range(2):
            lb[pp * 2 + a] = whole[a * SPAN : (a + 1) * SPAN]
            copy = final_copy(pair * 2 + a, pp * 2 + a, pp * 2 + a)
            copy.start()
            final_sent.append(copy)

    total = sums[own_index]
    for k, (yy, tt) in enumerate(peers):
        index = yy * 4 + tt
        remote(sums.at[index], sums.at[index], q_ss.at[k], q_rs.at[index], z_partner).wait_recv()
        total = total + sums[index]
    mean[...] = total * (1.0 / D)
    for b in range(2):
        copy = remote(mean, means.at[h], m_ss.at[b], m_rs.at[h], device(1 - pool, x, y, b, t))
        copy.start()
        sum_sent.append(copy)

    for s in range(4):
        remote(lb.at[s], st.at[s], f_ss.at[s], f_rs.at[s], z_partner).wait_recv()
        put(s, every, st[s].astype(jnp.float32))

    def lay_out(at):
        @pl.when(zero_pool)
        def _():
            for s in range(4):
                quarter = [get(s, every_fourth(k)) for k in range(4)]
                tiles[at, s * (SPAN // 4) : (s + 1) * (SPAN // 4), :] = jnp.concatenate(
                    quarter, axis=1
                ).astype(jnp.bfloat16)

        @pl.when(jnp.logical_not(zero_pool))
        def _():
            tiles[at] = jnp.concatenate([get(s, every) for s in range(4)], axis=1).astype(jnp.bfloat16)

    lay_out(0)
    stream_out = pltpu.make_async_copy(tiles.at[0], stream_hbm.at[0], out_sem.at[0])
    stream_out.start()
    gains = [gain_ref[:, r * PIECE : (r + 1) * PIECE] for r in range(4)]

    def gain_at(s):
        return jnp.where(zero_pool, ylo * 2 + h, s)

    ones = jnp.ones((8, PIECE), jnp.float32)
    sub = lax.broadcasted_iota(jnp.int32, (8, SPAN), 0)
    scales = []
    for b in range(2):
        remote(mean, means.at[b], m_ss.at[b], m_rs.at[b], z_partner).wait_recv()
        scales.append(lax.rsqrt(means[b] + EPSILON))
    for s in range(4):
        from_h = jnp.where(zero_pool, s % 2, h)
        from_a = jnp.where(zero_pool, s // 2, ylo)
        picked = jnp.where(from_h == 0, scales[0], scales[1])
        picked = jnp.where(from_a == 0, picked[:, :SPAN], picked[:, SPAN:])
        picked = jnp.where(sub == yhi, picked, 0.0)
        wide = lax.dot_general(
            picked, ones, (((0,), (0,)), ((), ())), preferred_element_type=jnp.float32,
            precision=lax.Precision.HIGHEST,
        )
        gain = gains[0]
        for r in range(4):
            gain = jnp.where(gain_at(s) == r, gains[r], gain)
        put(s, every, get(s, every) * wide * gain)
    lay_out(1)
    normed_out = pltpu.make_async_copy(tiles.at[1], normed_hbm.at[0], out_sem.at[1])
    normed_out.start()

    for copy in w_over + [pass_first, pass_second] + w_first + w_second + first_a + second_a + p1_sent + p2_sent + final_sent + sum_sent:
        copy.wait_send()
    for s in range(4):
        keeps, near, far = res_copies(s)

        @pl.when(jnp.logical_not(keeps))
        def _():
            far.wait_send()

    stream_out.wait()
    normed_out.wait()


def fused(plen, slen, q, k, v, sk, sv, res, w, gain):
    smem = pl.BlockSpec(memory_space=pltpu.SMEM)
    vmem = pl.BlockSpec(memory_space=pltpu.VMEM)
    hbm = pl.BlockSpec(memory_space=pl.ANY)
    dma = pltpu.SemaphoreType.DMA
    bf, f32 = jnp.bfloat16, jnp.float32
    out = jax.ShapeDtypeStruct((1, SPAN, 2 * HALF), bf)
    return pl.pallas_call(
        body,
        out_shape=(out, out),
        in_specs=[smem, smem] + [hbm] * 7 + [vmem],
        out_specs=(hbm, hbm),
        scratch_shapes=[
            pltpu.VMEM((SPAN, 2 * HALF), bf),
            pltpu.VMEM((PREFIX, KVL * HD), bf),
            pltpu.VMEM((PREFIX, KVL * HD), bf),
            pltpu.VMEM((SPAN, KVL * HD), bf),
            pltpu.VMEM((SPAN, KVL * HD), bf),
            pltpu.VMEM((SPAN, 2 * HALF), bf),
            pltpu.VMEM((4, 3, SPAN, HD), f32),
            pltpu.VMEM((4, SPAN, PIECE), bf),
            pltpu.VMEM((2, SPAN, 2 * HALF), bf),
            pltpu.VMEM((KVL, ROWS, HD), bf),
            pltpu.VMEM((3, ROWS, KEY_BLOCK), f32),
            pltpu.VMEM((KVL, ROWS, SPAN), f32),
            pltpu.VMEM((KVL, ROWS, HD), f32),
            pltpu.VMEM((KVL, ROWS, 2 * HD), f32),
            pltpu.VMEM((KVL, PREFIX, 2 * HD), bf),
            pltpu.VMEM((KVL, SPAN, 2 * HD), bf),
            pltpu.VMEM((2, 4 * WCOLS, 2 * HALF), bf),
            pltpu.VMEM((KVL, 4 * SPAN, HALF), bf),
            pltpu.VMEM((4, 4 * WCOLS, 2 * SPAN), f32),
            pltpu.VMEM((4, 4 * WCOLS, 2 * SPAN), bf),
            pltpu.VMEM((2, 4, WCOLS, 2 * SPAN), bf),
            pltpu.VMEM((4, WCOLS, 2 * SPAN), bf),
            pltpu.VMEM((4, WCOLS, 2 * SPAN), bf),
            pltpu.VMEM((4, SPAN, PIECE), bf),
            pltpu.VMEM((2, PIECE + 64, 2 * SPAN), f32),
            pltpu.VMEM((PIECE + 64, 2 * SPAN), f32),
            pltpu.VMEM((4, SPAN, PIECE), bf),
            pltpu.VMEM((4, SPAN, PIECE), bf),
            pltpu.VMEM((16, 8, 2 * SPAN), f32),
            pltpu.VMEM((8, 2 * SPAN), f32),
            pltpu.VMEM((2, 8, 2 * SPAN), f32),
            dma((5 + BLOCKS,)),
            dma,
            dma((2,)),
            dma((2, 2, 3)),
            dma((2, 4, 2)),
            dma((KVL, 3)),
            dma((KVL, 4)),
            dma((4,)),
            dma((4,)),
            dma((4, 2)),
            dma((2, 4)),
            dma((4,)),
            dma((4,)),
            dma((4,)),
            dma((4,)),
            dma((16,)),
            dma((16,)),
            dma((2,)),
            dma((2,)),
            dma((2,)),
        ],
        compiler_params=pltpu.CompilerParams(
            has_side_effects=True, collective_id=0, vmem_limit_bytes=62 << 20
        ),
        name="fused",
    )(plen, slen, q, k, v, sk, sv, res, w, gain)


def shards(
    queries, new_keys, new_values, cache_keys, cache_values, prefix_len, span_len, residual, out_proj,
    norm_gain,
):
    return fused(
        prefix_len, span_len, queries[0], cache_keys[0, 0], cache_values[0, 0], new_keys[0],
        new_values[0], residual[0], jnp.swapaxes(out_proj[0], 0, 1), norm_gain,
    )


def solution(mesh):
    placed = (
        P("pool", "group", "tensor"),
        P("pool", "group", "tensor"),
        P("pool", "group", "tensor"),
        P("pool", "group", None, "tensor"),
        P("pool", "group", None, "tensor"),
        P("pool", "group"),
        P("pool", "group"),
        P("pool", "group", "tensor"),
        P("pool", "tensor", "group"),
        P("pool", "tensor"),
    )
    return jax.shard_map(
        shards,
        mesh=mesh,
        in_specs=placed,
        out_specs=(P("pool", "group", "tensor"), P("pool", "group", "tensor")),
        check_vma=False,
    )
```

```python
import functools
import math

import jax
import jax.numpy as jnp
from jax import lax
from jax.experimental import pallas as pl
from jax.experimental.pallas import tpu as pltpu
from jax.sharding import PartitionSpec as P

D = 5120
HD = 128
KVL = 2
GROUP_HEADS = 5
PREFIX = 4096
SPAN = 192
ROWS = GROUP_HEADS * SPAN
HALF = GROUP_HEADS * HD
EPSILON = 1e-6
KEY_BLOCK = 2048
BLOCKS = PREFIX // KEY_BLOCK
PIECE = 320
WCOLS = 160
WHALF = 80
LOG2 = math.log2(math.e) / math.sqrt(HD)
MASKED = -1e30
MESH = pl.DeviceIdType.MESH


def nt(a, b, precision=None):
    return lax.dot_general(
        a, b, (((1,), (1,)), ((), ())), preferred_element_type=jnp.float32, precision=precision
    )


def body(
    plen_ref, slen_ref, q_hbm, k_hbm, v_hbm, sk_hbm, sv_hbm, res_hbm, w_hbm, gain_ref,
    stream_hbm, normed_hbm,
    q_ref, k_ref, v_ref, sk_ref, sv_ref, res_ref, p32, rp, tiles,
    qs, S, Sp, mx, acc, va, vas,
    wg, ag, pr, pb, rcv1, s2, rcv2, rres, rt, turn, lb, st, mid, sums, mean, means,
    in_sem, w_loc, w_zs, w_xs, w_rs, a_ss, a_rs, res_ss, res_rs,
    p1_ss, p1_rs, p2_ss, p2_rs, f_ss, f_rs, g_ss, g_rs, q_ss, q_rs, m_ss, m_rs, out_sem,
):
    pool = lax.axis_index("pool")
    group = lax.axis_index("group")
    t = lax.axis_index("tensor")
    h = lax.rem(group, 2)
    y = lax.rem(lax.div(group, 2), 4)
    x = lax.div(group, 8)
    ylo = lax.rem(y, 2)
    yhi = lax.div(y, 2)
    zero_pool = pool == 0

    def device(px, xx, yy, hh, tt):
        return (px, (xx * 4 + yy) * 2 + hh, tt)

    def remote(src, dst, send, recv, where):
        return pltpu.make_async_remote_copy(
            src_ref=src, dst_ref=dst, send_sem=send, recv_sem=recv, device_id=where,
            device_id_type=MESH,
        )

    barrier = pltpu.get_barrier_semaphore()
    peers = [
        (lax.rem(y + k // 4, 4), lax.rem(t + k % 4, 4)) for k in range(1, 16)
    ]
    friends = [device(pool, x, yy, h, tt) for yy, tt in peers]
    friends += [device(pool, x, a, 1 - h, t) for a in range(4)]
    friends += [device(pool, lax.rem(x + k, 4), y, h, t) for k in (1, 2, 3)]
    friends += [device(1 - pool, x, a, b, t) for a in range(4) for b in range(2)]
    for friend in friends:
        pl.semaphore_signal(barrier, 1, device_id=friend, device_id_type=MESH)

    def put(s, rows, value):
        blank = jnp.zeros((value.shape[0], 3 * HD - PIECE), jnp.float32)
        full = jnp.concatenate([value, blank], axis=1)
        for c in range(3):
            p32[s, c, rows, :] = full[:, c * HD : (c + 1) * HD]

    def get(s, rows):
        full = jnp.concatenate([p32[s, c, rows, :] for c in range(3)], axis=1)
        return full[:, :PIECE]

    every = slice(0, SPAN)

    def every_fourth(k):
        return pl.ds(k, SPAN // 4, stride=4)


    def load(src, dst, index):
        copy = pltpu.make_async_copy(src, dst, in_sem.at[index])
        copy.start()
        return copy

    load_q = load(q_hbm, q_ref, 0)
    load_sk = load(sk_hbm, sk_ref, 1)
    load_sv = load(sv_hbm, sv_ref, 2)
    load_k = [
        load(k_hbm.at[pl.ds(j * KEY_BLOCK, KEY_BLOCK)], k_ref.at[pl.ds(j * KEY_BLOCK, KEY_BLOCK)], 3 + j)
        for j in range(BLOCKS)
    ]
    load_v = load(v_hbm, v_ref, 3 + BLOCKS)
    load_res = load(res_hbm, res_ref, 4 + BLOCKS)

    sums[y * 4 + t] = jnp.zeros((8, 2 * SPAN), jnp.float32)

    def w_half(hh, xx, part):
        return wg.at[hh, pl.ds(pl.multiple_of(xx * WCOLS + part * WHALF, 16), WHALF)]

    def w_from(part):
        return w_hbm.at[pl.ds(part * WHALF, WHALF)]

    z_partner = device(pool, x, y, 1 - h, t)
    x_up, x_down, x_far = lax.rem(x + 1, 4), lax.rem(x + 3, 4), lax.rem(x + 2, 4)
    own_w = pltpu.make_async_copy(
        w_hbm, wg.at[h, pl.ds(pl.multiple_of(x * WCOLS, WCOLS), WCOLS)], w_loc
    )
    own_w.start()
    w_over = [
        remote(w_from(part), w_half(h, x, part), w_zs.at[part], w_rs.at[h, x, part], z_partner)
        for part in range(2)
    ]

    def w_send(source, hh, xx, part, wave, way, to_x):
        return remote(
            source, w_half(hh, xx, part), w_xs.at[wave, part, way], w_rs.at[hh, xx, part],
            device(pool, to_x, y, h, t),
        )

    def w_direct(wave):
        hh = h if wave == 0 else 1 - h
        out = []
        for part in range(2):
            source = w_from(part) if wave == 0 else w_half(hh, x, part)
            ways = [(0, x_up), (1, x_down)]
            for way, to_x in ways if part == 0 else ways[::-1]:
                out.append(w_send(source, hh, x, part, wave, way, to_x))
        return out

    def w_onward(wave):
        hh = h if wave == 0 else 1 - h
        return [
            w_send(w_half(hh, x_down, 0), hh, x_down, 0, wave, 2, x_up),
            w_send(w_half(hh, x_up, 1), hh, x_up, 1, wave, 2, x_down),
        ]

    def w_wait(hh, xx, part):
        remote(
            w_half(hh, xx, part), w_half(hh, xx, part), w_zs.at[0], w_rs.at[hh, xx, part], z_partner
        ).wait_recv()

    def pass_on(wave):
        hh = h if wave == 0 else 1 - h
        copies = w_onward(wave)
        w_wait(hh, x_down, 0)
        copies[0].start()
        w_wait(hh, x_up, 1)
        copies[1].start()
        return copies

    def w_rest(hh):
        w_wait(hh, x_down, 1)
        w_wait(hh, x_up, 0)
        w_wait(hh, x_far, 0)
        w_wait(hh, x_far, 1)

    def res_plan(s):
        to_y = jnp.where(zero_pool, ylo * 2 + h, s)
        to_h = jnp.where(zero_pool, s % 2, h)
        slot = jnp.where(zero_pool, yhi * 2 + s // 2, y)
        keeps = jnp.logical_and(to_y == y, to_h == h)
        return keeps, slot, device(pool, x, to_y, to_h, t)

    def res_copies(s):
        keeps, slot, where = res_plan(s)
        near = pltpu.make_async_copy(rp.at[s], rres.at[slot], res_rs.at[slot])
        far = remote(rp.at[s], rres.at[slot], res_ss.at[s], res_rs.at[slot], where)
        return keeps, near, far

    plen = plen_ref[0, 0]
    slen = slen_ref[0, 0]
    row_at = lax.broadcasted_iota(jnp.int32, (SPAN, SPAN), 0)
    col_at = lax.broadcasted_iota(jnp.int32, (SPAN, SPAN), 1)
    span_mask = (col_at <= row_at) & (col_at < slen)

    def head_rows(g):
        return slice(g * SPAN, (g + 1) * SPAN)

    def head_cols(hd, g):
        return slice((hd * GROUP_HEADS + g) * HD, (hd * GROUP_HEADS + g + 1) * HD)

    def span_scores(hd):
        for g in range(GROUP_HEADS):
            s = nt(qs[hd, head_rows(g), :], sk_ref[:, hd * HD : (hd + 1) * HD])
            s = jnp.where(span_mask, s, MASKED)
            Sp[hd, head_rows(g), :] = s
            rest = s[:, HD:]
            mx[hd, head_rows(g), :] = jnp.maximum(
                s[:, :HD], jnp.concatenate([rest, rest], axis=1)
            )

    def scores(hd, j):
        base = pl.multiple_of(j * KEY_BLOCK, KEY_BLOCK)
        keys = k_ref[pl.ds(base, KEY_BLOCK), hd * HD : (hd + 1) * HD]
        position = base + lax.broadcasted_iota(jnp.int32, (1, KEY_BLOCK), 1)
        bias = jnp.where(position < plen, 0.0, MASKED)
        slot = lax.rem(hd * BLOCKS + j, 3)
        for g in range(GROUP_HEADS):
            s = nt(qs[hd, head_rows(g), :], keys) + bias
            S[slot, head_rows(g), :] = s
            m = mx[hd, head_rows(g), :]
            for u in range(0, KEY_BLOCK, HD):
                m = jnp.maximum(m, s[:, u : u + HD])
            mx[hd, head_rows(g), :] = m

    def finish_max(hd):
        m = jnp.max(mx[hd], axis=1, keepdims=True) * LOG2
        mx[hd] = jnp.broadcast_to(m, (ROWS, HD))

    def weigh(hd, j):
        base = pl.multiple_of(j * KEY_BLOCK, KEY_BLOCK)
        values = va[hd, pl.ds(base, KEY_BLOCK), :]
        slot = lax.rem(hd * BLOCKS + j, 3)
        for g in range(GROUP_HEADS):
            m = mx[hd, head_rows(g), :]
            wide = jnp.concatenate([m] * (KEY_BLOCK // HD), axis=1)
            p = jnp.exp2(S[slot, head_rows(g), :] * LOG2 - wide).astype(jnp.bfloat16)
            acc[hd, head_rows(g), :] += jnp.dot(p, values, preferred_element_type=jnp.float32)

    def span_weigh(hd):
        for g in range(GROUP_HEADS):
            m = mx[hd, head_rows(g), :]
            wide = jnp.concatenate([m, m[:, : SPAN - HD]], axis=1)
            p = jnp.exp2(Sp[hd, head_rows(g), :] * LOG2 - wide).astype(jnp.bfloat16)
            acc[hd, head_rows(g), :] = jnp.dot(p, vas[hd], preferred_element_type=jnp.float32)

    def a_slot(hd, yy):
        return ag.at[hd, pl.ds(pl.multiple_of(yy * SPAN, SPAN), SPAN)]

    def attended(hd):
        for g in range(GROUP_HEADS):
            a = acc[hd, head_rows(g), :]
            out = (a[:, :HD] / a[:, HD:]).astype(jnp.bfloat16)
            ag[hd, pl.ds(pl.multiple_of(y * SPAN, SPAN), SPAN), g * HD : (g + 1) * HD] = out

    y_partners = [yhi * 2 + 1 - ylo, (1 - yhi) * 2 + ylo, (1 - yhi) * 2 + 1 - ylo]

    y_up, y_down = lax.rem(y + 1, 4), lax.rem(y + 3, 4)

    def a_copy(hd, yy, i, to_y):
        return remote(a_slot(hd, yy), a_slot(hd, yy), a_ss.at[hd, i], a_rs.at[hd, yy], device(pool, x, to_y, h, t))

    def a_copies(hd):
        return [a_copy(hd, y, 0, y_up), a_copy(hd, y, 1, y_down)]

    def a_arrival(hd, yy):
        return remote(a_slot(hd, yy), a_slot(hd, yy), a_ss.at[hd, 0], a_rs.at[hd, yy], z_partner)

    pl.semaphore_wait(barrier, len(friends))
    w_first = w_direct(0)
    for copy in w_over + w_first:
        copy.start()
    load_q.wait()
    for hd in range(KVL):
        for g in range(GROUP_HEADS):
            qs[hd, head_rows(g), :] = q_ref[:, head_cols(hd, g)]
    load_sk.wait()
    span_scores(0)
    for copy in load_k:
        copy.wait()
    pl.loop(0, BLOCKS)(lambda j: scores(0, j))
    load_v.wait()
    load_sv.wait()
    for hd in range(KVL):
        va[hd, :, :HD] = v_ref[:, hd * HD : (hd + 1) * HD]
        va[hd, :, HD:] = jnp.ones((PREFIX, HD), jnp.bfloat16)
        vas[hd, :, :HD] = sv_ref[:, hd * HD : (hd + 1) * HD]
        vas[hd, :, HD:] = jnp.ones((SPAN, HD), jnp.bfloat16)
    finish_max(0)
    span_weigh(0)
    span_scores(1)

    def middle(j):
        weigh(0, j)
        scores(1, j)

    pl.loop(0, BLOCKS)(middle)
    attended(0)
    first_a = a_copies(0)
    for copy in first_a:
        copy.start()
    w_first += pass_on(0)
    finish_max(1)
    span_weigh(1)
    pl.loop(0, BLOCKS)(lambda j: weigh(1, j))
    attended(1)
    second_a = a_copies(1)
    for copy in second_a:
        copy.start()

    w_second = w_direct(1)
    for part in range(2):
        w_wait(1 - h, x, part)
        for copy in w_second[2 * part : 2 * part + 2]:
            copy.start()
    a_arrival(1, y_up).wait_recv()
    pass_second = a_copy(1, y_up, 2, y_down)
    pass_second.start()
    a_arrival(0, y_down).wait_recv()
    pass_first = a_copy(0, y_down, 2, y_up)
    pass_first.start()

    load_res.wait()

    @pl.when(zero_pool)
    def _():
        for s in range(4):
            rows = res_ref[s * (SPAN // 4) : (s + 1) * (SPAN // 4), :].astype(jnp.float32)
            for k in range(4):
                put(s, every_fourth(k), rows[:, k * PIECE : (k + 1) * PIECE])

    @pl.when(jnp.logical_not(zero_pool))
    def _():
        for s in range(4):
            put(s, every, res_ref[:, s * PIECE : (s + 1) * PIECE].astype(jnp.float32))

    for s in range(4):
        rp[s] = get(s, every).astype(jnp.bfloat16)
        keeps, near, far = res_copies(s)

        @pl.when(keeps)
        def _():
            near.start()

        @pl.when(jnp.logical_not(keeps))
        def _():
            far.start()

    t1 = t + 1 - 2 * lax.rem(t, 2)
    t2 = lax.rem(t + 2, 4)
    t3 = 3 - t
    tpar = lax.rem(t, 2)
    thi = lax.div(t, 2)

    def piece_rows(piece):
        return pl.ds(pl.multiple_of(piece * WCOLS, WCOLS), WCOLS)

    def p1_copy(u, i, piece):
        return remote(
            pb.at[u, piece_rows(piece)], rcv1.at[lax.div(piece, 2), u], p1_ss.at[u, i],
            p1_rs.at[lax.div(piece, 2), u], device(pool, x, y, h, t1),
        )

    def p1_arrival(jj, u):
        return remote(rcv1.at[jj, u], rcv1.at[jj, u], p1_ss.at[u, 0], p1_rs.at[jj, u], z_partner)

    def p2_copy(u):
        return remote(s2.at[u], rcv2.at[u], p2_ss.at[u], p2_rs.at[u], device(pool, x, y, h, t2))

    def unit(u):
        hh = h if u < 2 else 1 - h
        pair = yhi if u % 2 == 0 else 1 - yhi
        rows = pl.ds(pl.multiple_of(pair * 2 * SPAN, 2 * SPAN), 2 * SPAN)
        total = nt(wg[hh, :, :HALF], ag[0, rows, :]) + nt(wg[hh, :, HALF:], ag[1, rows, :])
        pr[u] = total
        pb[u] = total.astype(jnp.bfloat16)
        copy = p1_copy(u, 0, t3)
        copy.start()
        return copy

    def last_part(u):
        copy = p1_copy(u, 1, t1)
        copy.start()
        return copy

    def second(u):
        p1_arrival(1 - thi, u).wait_recv()
        total = pr[u, piece_rows(t2), :] + rcv1[1 - thi, u].astype(jnp.float32)
        s2[u] = total.astype(jnp.bfloat16)
        copy = p2_copy(u)
        copy.start()
        return copy

    p1_sent = []
    p2_sent = []
    own_w.wait()
    w_rest(h)
    first_head = jnp.where(ylo == 0, 0, 1)
    a_arrival(first_head, y_partners[0]).wait_recv()
    p1_sent.append(unit(0))
    p1_sent.append(last_part(0))
    w_second += pass_on(1)
    a_arrival(1 - first_head, y_partners[2]).wait_recv()
    for hd in range(KVL):
        a_arrival(hd, y_partners[1]).wait_recv()
    p1_sent.append(unit(1))
    p2_sent.append(second(0))
    p1_sent.append(last_part(1))
    p2_sent.append(second(1))

    for pair in range(2):
        for a in range(2):
            at = pair * 2 + a
            pltpu.make_async_copy(rres.at[at], rres.at[at], res_rs.at[at]).wait()
        both = jnp.concatenate([rres[pair * 2], rres[pair * 2 + 1]], axis=0).astype(jnp.float32)
        blank = jnp.zeros((2 * SPAN, 3 * HD - PIECE), jnp.float32)
        rt[pair] = jnp.transpose(jnp.concatenate([both, blank], axis=1))

    w_rest(1 - h)
    p1_sent.append(unit(2))
    p1_sent.append(unit(3))
    p2_sent.append(second(2))
    p1_sent.append(last_part(2))
    p2_sent.append(second(3))
    p1_sent.append(last_part(3))

    def final_copy(s, slot_from, index):
        to_y = jnp.where(zero_pool, s, lax.div(s, 2) * 2 + yhi)
        to_h = jnp.where(zero_pool, h, ylo)
        slot = jnp.where(zero_pool, y, lax.rem(s, 2) * 2 + h)
        return remote(
            lb.at[slot_from], st.at[slot], f_ss.at[index], f_rs.at[slot],
            device(1 - pool, x, to_y, to_h, t),
        )

    def detour(s, slot_from, index):
        to_y = lax.div(s, 2) * 2 + yhi
        crosses = jnp.logical_and(jnp.logical_not(zero_pool), h != ylo)
        part = lax.rem(s, 2)
        copy = remote(
            lb.at[slot_from], mid.at[part], f_ss.at[index], g_rs.at[part],
            device(pool, x, to_y, h, t),
        )
        return jnp.logical_and(crosses, to_y != y), copy

    carries = jnp.logical_and(jnp.logical_not(zero_pool), ylo * 2 + 1 - h != y)

    def carried(a):
        return remote(
            mid.at[a], st.at[a * 2 + h], g_ss.at[a], f_rs.at[a * 2 + h],
            device(1 - pool, x, y, 1 - h, t),
        )

    turn[pl.ds(PIECE, 64), :] = jnp.zeros((64, 2 * SPAN), jnp.float32)
    own_index = y * 4 + t
    final_sent = []
    sum_sent = []
    for pp in range(2):
        pair = yhi if pp == 0 else 1 - yhi
        squares = jnp.zeros((1, 2 * SPAN), jnp.float32)
        for hh in range(2):
            u = hh * 2 + pp
            at = h if hh == 0 else 1 - h
            p1_arrival(thi, u).wait_recv()
            p2_copy(u).wait_recv()
            rows = pl.ds(pl.multiple_of(at * WCOLS, WCOLS), WCOLS)
            total = (
                pr[u, piece_rows(t), :]
                + rcv1[thi, u].astype(jnp.float32)
                + rcv2[u].astype(jnp.float32)
                + rt[pair, rows, :]
            )
            total = total.astype(jnp.bfloat16).astype(jnp.float32)
            turn[rows, :] = total
            squares = squares + jnp.sum(total * total, axis=0, keepdims=True)
        sums[own_index, pl.ds(pair, 1), :] = squares
        if pp == 1:
            for k, (yy, tt) in enumerate(peers):
                copy = remote(
                    sums.at[own_index], sums.at[own_index], q_ss.at[k], q_rs.at[own_index],
                    device(pool, x, yy, h, tt),
                )
                copy.start()
                sum_sent.append(copy)
        whole = jnp.transpose(turn[...])[:, :PIECE].astype(jnp.bfloat16)
        for a in range(2):
            lb[pp * 2 + a] = whole[a * SPAN : (a + 1) * SPAN]
            copy = final_copy(pair * 2 + a, pp * 2 + a, pp * 2 + a)
            hops, around = detour(pair * 2 + a, pp * 2 + a, pp * 2 + a)

            @pl.when(hops)
            def _():
                around.start()

            @pl.when(jnp.logical_not(hops))
            def _():
                copy.start()

            final_sent.append(copy)

    @pl.when(carries)
    def _():
        for a in range(2):
            remote(mid.at[a], mid.at[a], g_ss.at[a], g_rs.at[a], z_partner).wait_recv()
            carried(a).start()

    total = sums[own_index]
    for k, (yy, tt) in enumerate(peers):
        index = yy * 4 + tt
        remote(sums.at[index], sums.at[index], q_ss.at[k], q_rs.at[index], z_partner).wait_recv()
        total = total + sums[index]
    mean[...] = total * (1.0 / D)
    for b in range(2):
        copy = remote(mean, means.at[h], m_ss.at[b], m_rs.at[h], device(1 - pool, x, y, b, t))
        copy.start()
        sum_sent.append(copy)

    for s in range(4):
        remote(lb.at[s], st.at[s], f_ss.at[s], f_rs.at[s], z_partner).wait_recv()
        put(s, every, st[s].astype(jnp.float32))

    def lay_out(at):
        @pl.when(zero_pool)
        def _():
            for s in range(4):
                quarter = [get(s, every_fourth(k)) for k in range(4)]
                tiles[at, s * (SPAN // 4) : (s + 1) * (SPAN // 4), :] = jnp.concatenate(
                    quarter, axis=1
                ).astype(jnp.bfloat16)

        @pl.when(jnp.logical_not(zero_pool))
        def _():
            tiles[at] = jnp.concatenate([get(s, every) for s in range(4)], axis=1).astype(jnp.bfloat16)

    lay_out(0)
    stream_out = pltpu.make_async_copy(tiles.at[0], stream_hbm.at[0], out_sem.at[0])
    stream_out.start()
    gains = [gain_ref[:, r * PIECE : (r + 1) * PIECE] for r in range(4)]

    def gain_at(s):
        return jnp.where(zero_pool, ylo * 2 + h, s)

    blank = jnp.zeros((1, 3 * HD - PIECE), jnp.float32)
    sub = lax.broadcasted_iota(jnp.int32, (8, 2 * SPAN), 0)
    scales = []
    for b in range(2):
        remote(mean, means.at[b], m_ss.at[b], m_rs.at[b], z_partner).wait_recv()
        scales.append(lax.rsqrt(means[b] + EPSILON))
    for s in range(4):
        from_h = jnp.where(zero_pool, s % 2, h)
        from_a = jnp.where(zero_pool, s // 2, ylo)
        picked = jnp.where(from_h == 0, scales[0], scales[1])
        row = jnp.sum(jnp.where(sub == yhi, picked, 0.0), axis=0, keepdims=True)
        row = jnp.where(from_a == 0, row[:, : 2 * HD], row[:, 2 * SPAN - 2 * HD :])
        turned = jnp.transpose(jnp.broadcast_to(row, (HD, 2 * HD)))
        wide = jnp.where(from_a == 0, turned[:SPAN], turned[2 * HD - SPAN :])
        gain = gains[0]
        for r in range(4):
            gain = jnp.where(gain_at(s) == r, gains[r], gain)
        gain = jnp.concatenate([gain, blank], axis=1)
        for c in range(3):
            p32[s, c] = p32[s, c] * wide * gain[:, c * HD : (c + 1) * HD]
    lay_out(1)
    normed_out = pltpu.make_async_copy(tiles.at[1], normed_hbm.at[0], out_sem.at[1])
    normed_out.start()

    @pl.when(carries)
    def _():
        for a in range(2):
            carried(a).wait_send()

    for copy in w_over + [pass_first, pass_second] + w_first + w_second + first_a + second_a + p1_sent + p2_sent + final_sent + sum_sent:
        copy.wait_send()
    for s in range(4):
        keeps, near, far = res_copies(s)

        @pl.when(jnp.logical_not(keeps))
        def _():
            far.wait_send()

    stream_out.wait()
    normed_out.wait()


def fused(plen, slen, q, k, v, sk, sv, res, w, gain):
    smem = pl.BlockSpec(memory_space=pltpu.SMEM)
    vmem = pl.BlockSpec(memory_space=pltpu.VMEM)
    hbm = pl.BlockSpec(memory_space=pl.ANY)
    dma = pltpu.SemaphoreType.DMA
    bf, f32 = jnp.bfloat16, jnp.float32
    out = jax.ShapeDtypeStruct((1, SPAN, 2 * HALF), bf)
    return pl.pallas_call(
        body,
        out_shape=(out, out),
        in_specs=[smem, smem] + [hbm] * 7 + [vmem],
        out_specs=(hbm, hbm),
        scratch_shapes=[
            pltpu.VMEM((SPAN, 2 * HALF), bf),
            pltpu.VMEM((PREFIX, KVL * HD), bf),
            pltpu.VMEM((PREFIX, KVL * HD), bf),
            pltpu.VMEM((SPAN, KVL * HD), bf),
            pltpu.VMEM((SPAN, KVL * HD), bf),
            pltpu.VMEM((SPAN, 2 * HALF), bf),
            pltpu.VMEM((4, 3, SPAN, HD), f32),
            pltpu.VMEM((4, SPAN, PIECE), bf),
            pltpu.VMEM((2, SPAN, 2 * HALF), bf),
            pltpu.VMEM((KVL, ROWS, HD), bf),
            pltpu.VMEM((3, ROWS, KEY_BLOCK), f32),
            pltpu.VMEM((KVL, ROWS, SPAN), f32),
            pltpu.VMEM((KVL, ROWS, HD), f32),
            pltpu.VMEM((KVL, ROWS, 2 * HD), f32),
            pltpu.VMEM((KVL, PREFIX, 2 * HD), bf),
            pltpu.VMEM((KVL, SPAN, 2 * HD), bf),
            pltpu.VMEM((2, 4 * WCOLS, 2 * HALF), bf),
            pltpu.VMEM((KVL, 4 * SPAN, HALF), bf),
            pltpu.VMEM((4, 4 * WCOLS, 2 * SPAN), f32),
            pltpu.VMEM((4, 4 * WCOLS, 2 * SPAN), bf),
            pltpu.VMEM((2, 4, WCOLS, 2 * SPAN), bf),
            pltpu.VMEM((4, WCOLS, 2 * SPAN), bf),
            pltpu.VMEM((4, WCOLS, 2 * SPAN), bf),
            pltpu.VMEM((4, SPAN, PIECE), bf),
            pltpu.VMEM((2, PIECE + 64, 2 * SPAN), f32),
            pltpu.VMEM((PIECE + 64, 2 * SPAN), f32),
            pltpu.VMEM((4, SPAN, PIECE), bf),
            pltpu.VMEM((4, SPAN, PIECE), bf),
            pltpu.VMEM((2, SPAN, PIECE), bf),
            pltpu.VMEM((16, 8, 2 * SPAN), f32),
            pltpu.VMEM((8, 2 * SPAN), f32),
            pltpu.VMEM((2, 8, 2 * SPAN), f32),
            dma((5 + BLOCKS,)),
            dma,
            dma((2,)),
            dma((2, 2, 3)),
            dma((2, 4, 2)),
            dma((KVL, 3)),
            dma((KVL, 4)),
            dma((4,)),
            dma((4,)),
            dma((4, 2)),
            dma((2, 4)),
            dma((4,)),
            dma((4,)),
            dma((4,)),
            dma((4,)),
            dma((2,)),
            dma((2,)),
            dma((16,)),
            dma((16,)),
            dma((2,)),
            dma((2,)),
            dma((2,)),
        ],
        compiler_params=pltpu.CompilerParams(
            has_side_effects=True, collective_id=0, vmem_limit_bytes=62 << 20
        ),
        name="fused",
    )(plen, slen, q, k, v, sk, sv, res, w, gain)


def copy_body(a, b, out_a, out_b):
    out_a[...] = a[...]
    out_b[...] = b[...]


def hand_over(stream, normed):
    block = pl.BlockSpec((1, SPAN // 2, 2 * HALF), lambda i: (0, i, 0))
    out = jax.ShapeDtypeStruct(stream.shape, stream.dtype)
    return pl.pallas_call(
        copy_body, grid=(2,), out_shape=(out, out), in_specs=[block, block],
        out_specs=(block, block), name="hand_over",
    )(stream, normed)


def shards(
    queries, new_keys, new_values, cache_keys, cache_values, prefix_len, span_len, residual, out_proj,
    norm_gain,
):
    return hand_over(*fused(
        prefix_len, span_len, queries[0], cache_keys[0, 0], cache_values[0, 0], new_keys[0],
        new_values[0], residual[0], jnp.swapaxes(out_proj[0], 0, 1), norm_gain,
    ))


def solution(mesh):
    placed = (
        P("pool", "group", "tensor"),
        P("pool", "group", "tensor"),
        P("pool", "group", "tensor"),
        P("pool", "group", None, "tensor"),
        P("pool", "group", None, "tensor"),
        P("pool", "group"),
        P("pool", "group"),
        P("pool", "group", "tensor"),
        P("pool", "tensor", "group"),
        P("pool", "tensor"),
    )
    return jax.shard_map(
        shards,
        mesh=mesh,
        in_specs=placed,
        out_specs=(P("pool", "group", "tensor"), P("pool", "group", "tensor")),
        check_vma=False,
    )
```

```python
import functools
import math

import jax
import jax.numpy as jnp
from jax import lax
from jax.experimental import pallas as pl
from jax.experimental.pallas import tpu as pltpu
from jax.sharding import PartitionSpec as P

D = 5120
HD = 128
KVL = 2
GROUP_HEADS = 5
PREFIX = 4096
SPAN = 192
ROWS = GROUP_HEADS * SPAN
HALF = GROUP_HEADS * HD
EPSILON = 1e-6
KEY_BLOCK = 2048
BLOCKS = PREFIX // KEY_BLOCK
PIECE = 320
WCOLS = 160
WHALF = 80
LOG2 = math.log2(math.e) / math.sqrt(HD)
MASKED = -1e30
MESH = pl.DeviceIdType.MESH


def nt(a, b, precision=None):
    return lax.dot_general(
        a, b, (((1,), (1,)), ((), ())), preferred_element_type=jnp.float32, precision=precision
    )


def body(
    plen_ref, slen_ref, q_hbm, k_hbm, v_hbm, sk_hbm, sv_hbm, res_hbm, w_hbm, gain_ref,
    stream_hbm, normed_hbm,
    q_ref, k_ref, v_ref, sk_ref, sv_ref, res_ref, p32, rp, tiles,
    qs, S, Sp, mx, acc, va, vas,
    wg, ag, pr, pb, rcv1, s2, rcv2, rres, rt, turn, lb, st, mid, sums, mean, means,
    in_sem, w_loc, w_zs, w_xs, w_rs, a_ss, a_rs, res_ss, res_rs,
    p1_ss, p1_rs, p2_ss, p2_rs, f_ss, f_rs, g_ss, g_rs, q_ss, q_rs, m_ss, m_rs, out_sem,
):
    pool = lax.axis_index("pool")
    group = lax.axis_index("group")
    t = lax.axis_index("tensor")
    h = lax.rem(group, 2)
    y = lax.rem(lax.div(group, 2), 4)
    x = lax.div(group, 8)
    ylo = lax.rem(y, 2)
    yhi = lax.div(y, 2)
    zero_pool = pool == 0

    def device(px, xx, yy, hh, tt):
        return (px, (xx * 4 + yy) * 2 + hh, tt)

    def remote(src, dst, send, recv, where):
        return pltpu.make_async_remote_copy(
            src_ref=src, dst_ref=dst, send_sem=send, recv_sem=recv, device_id=where,
            device_id_type=MESH,
        )

    barrier = pltpu.get_barrier_semaphore()
    peers = [
        (lax.rem(y + k // 4, 4), lax.rem(t + k % 4, 4)) for k in range(1, 16)
    ]
    friends = [device(pool, x, yy, h, tt) for yy, tt in peers]
    friends += [device(pool, x, a, 1 - h, t) for a in range(4)]
    friends += [device(pool, lax.rem(x + k, 4), y, h, t) for k in (1, 2, 3)]
    friends += [device(1 - pool, x, a, b, t) for a in range(4) for b in range(2)]
    for friend in friends:
        pl.semaphore_signal(barrier, 1, device_id=friend, device_id_type=MESH)

    def put(s, rows, value):
        blank = jnp.zeros((value.shape[0], 3 * HD - PIECE), jnp.float32)
        full = jnp.concatenate([value, blank], axis=1)
        for c in range(3):
            p32[s, c, rows, :] = full[:, c * HD : (c + 1) * HD]

    def get(s, rows):
        full = jnp.concatenate([p32[s, c, rows, :] for c in range(3)], axis=1)
        return full[:, :PIECE]

    every = slice(0, SPAN)

    def every_fourth(k):
        return pl.ds(k, SPAN // 4, stride=4)


    def load(src, dst, index):
        copy = pltpu.make_async_copy(src, dst, in_sem.at[index])
        copy.start()
        return copy

    load_q = load(q_hbm, q_ref, 0)
    load_sk = load(sk_hbm, sk_ref, 1)
    load_sv = load(sv_hbm, sv_ref, 2)
    load_k = [
        load(k_hbm.at[pl.ds(j * KEY_BLOCK, KEY_BLOCK)], k_ref.at[pl.ds(j * KEY_BLOCK, KEY_BLOCK)], 3 + j)
        for j in range(BLOCKS)
    ]
    load_v = load(v_hbm, v_ref, 3 + BLOCKS)
    load_res = load(res_hbm, res_ref, 4 + BLOCKS)

    sums[y * 4 + t] = jnp.zeros((8, 2 * SPAN), jnp.float32)

    def w_half(hh, xx, part):
        return wg.at[hh, pl.ds(pl.multiple_of(xx * WCOLS + part * WHALF, 16), WHALF)]

    def w_from(part):
        return w_hbm.at[pl.ds(part * WHALF, WHALF)]

    z_partner = device(pool, x, y, 1 - h, t)
    x_up, x_down, x_far = lax.rem(x + 1, 4), lax.rem(x + 3, 4), lax.rem(x + 2, 4)
    own_w = pltpu.make_async_copy(
        w_hbm, wg.at[h, pl.ds(pl.multiple_of(x * WCOLS, WCOLS), WCOLS)], w_loc
    )
    own_w.start()
    w_over = [
        remote(w_from(part), w_half(h, x, part), w_zs.at[part], w_rs.at[h, x, part], z_partner)
        for part in range(2)
    ]

    def w_send(source, hh, xx, part, wave, way, to_x):
        return remote(
            source, w_half(hh, xx, part), w_xs.at[wave, part, way], w_rs.at[hh, xx, part],
            device(pool, to_x, y, h, t),
        )

    def w_direct(wave):
        hh = h if wave == 0 else 1 - h
        out = []
        for part in range(2):
            source = w_from(part) if wave == 0 else w_half(hh, x, part)
            ways = [(0, x_up), (1, x_down)]
            for way, to_x in ways if part == 0 else ways[::-1]:
                out.append(w_send(source, hh, x, part, wave, way, to_x))
        return out

    def w_onward(wave):
        hh = h if wave == 0 else 1 - h
        return [
            w_send(w_half(hh, x_down, 0), hh, x_down, 0, wave, 2, x_up),
            w_send(w_half(hh, x_up, 1), hh, x_up, 1, wave, 2, x_down),
        ]

    def w_wait(hh, xx, part):
        remote(
            w_half(hh, xx, part), w_half(hh, xx, part), w_zs.at[0], w_rs.at[hh, xx, part], z_partner
        ).wait_recv()

    def pass_on(wave):
        hh = h if wave == 0 else 1 - h
        copies = w_onward(wave)
        w_wait(hh, x_down, 0)
        copies[0].start()
        w_wait(hh, x_up, 1)
        copies[1].start()
        return copies

    def w_rest(hh):
        w_wait(hh, x_down, 1)
        w_wait(hh, x_up, 0)
        w_wait(hh, x_far, 0)
        w_wait(hh, x_far, 1)

    def res_plan(s):
        to_y = jnp.where(zero_pool, ylo * 2 + h, s)
        to_h = jnp.where(zero_pool, s % 2, h)
        slot = jnp.where(zero_pool, yhi * 2 + s // 2, y)
        keeps = jnp.logical_and(to_y == y, to_h == h)
        return keeps, slot, device(pool, x, to_y, to_h, t)

    def res_copies(s):
        keeps, slot, where = res_plan(s)
        near = pltpu.make_async_copy(rp.at[s], rres.at[slot], res_rs.at[slot])
        far = remote(rp.at[s], rres.at[slot], res_ss.at[s], res_rs.at[slot], where)
        return keeps, near, far

    plen = plen_ref[0, 0]
    slen = slen_ref[0, 0]
    row_at = lax.broadcasted_iota(jnp.int32, (SPAN, SPAN), 0)
    col_at = lax.broadcasted_iota(jnp.int32, (SPAN, SPAN), 1)
    span_mask = (col_at <= row_at) & (col_at < slen)

    def head_rows(g):
        return slice(g * SPAN, (g + 1) * SPAN)

    def head_cols(hd, g):
        return slice((hd * GROUP_HEADS + g) * HD, (hd * GROUP_HEADS + g + 1) * HD)

    def span_scores(hd):
        for g in range(GROUP_HEADS):
            s = nt(qs[hd, head_rows(g), :], sk_ref[:, hd * HD : (hd + 1) * HD])
            s = jnp.where(span_mask, s, MASKED)
            Sp[hd, head_rows(g), :] = s
            rest = s[:, HD:]
            mx[hd, head_rows(g), :] = jnp.maximum(
                s[:, :HD], jnp.concatenate([rest, rest], axis=1)
            )

    def scores(hd, j):
        base = pl.multiple_of(j * KEY_BLOCK, KEY_BLOCK)
        keys = k_ref[pl.ds(base, KEY_BLOCK), hd * HD : (hd + 1) * HD]
        position = base + lax.broadcasted_iota(jnp.int32, (1, KEY_BLOCK), 1)
        bias = jnp.where(position < plen, 0.0, MASKED)
        slot = lax.rem(hd * BLOCKS + j, 3)
        for g in range(GROUP_HEADS):
            s = nt(qs[hd, head_rows(g), :], keys) + bias
            S[slot, head_rows(g), :] = s
            m = mx[hd, head_rows(g), :]
            for u in range(0, KEY_BLOCK, HD):
                m = jnp.maximum(m, s[:, u : u + HD])
            mx[hd, head_rows(g), :] = m

    def finish_max(hd):
        m = jnp.max(mx[hd], axis=1, keepdims=True) * LOG2
        mx[hd] = jnp.broadcast_to(m, (ROWS, HD))

    def weigh(hd, j):
        base = pl.multiple_of(j * KEY_BLOCK, KEY_BLOCK)
        values = va[hd, pl.ds(base, KEY_BLOCK), :]
        slot = lax.rem(hd * BLOCKS + j, 3)
        for g in range(GROUP_HEADS):
            m = mx[hd, head_rows(g), :]
            wide = jnp.concatenate([m] * (KEY_BLOCK // HD), axis=1)
            p = jnp.exp2(S[slot, head_rows(g), :] * LOG2 - wide).astype(jnp.bfloat16)
            acc[hd, head_rows(g), :] += jnp.dot(p, values, preferred_element_type=jnp.float32)

    def span_weigh(hd):
        for g in range(GROUP_HEADS):
            m = mx[hd, head_rows(g), :]
            wide = jnp.concatenate([m, m[:, : SPAN - HD]], axis=1)
            p = jnp.exp2(Sp[hd, head_rows(g), :] * LOG2 - wide).astype(jnp.bfloat16)
            acc[hd, head_rows(g), :] = jnp.dot(p, vas[hd], preferred_element_type=jnp.float32)

    def a_slot(hd, yy):
        return ag.at[hd, pl.ds(pl.multiple_of(yy * SPAN, SPAN), SPAN)]

    def attended(hd):
        for g in range(GROUP_HEADS):
            a = acc[hd, head_rows(g), :]
            out = (a[:, :HD] / a[:, HD:]).astype(jnp.bfloat16)
            ag[hd, pl.ds(pl.multiple_of(y * SPAN, SPAN), SPAN), g * HD : (g + 1) * HD] = out

    y_partners = [yhi * 2 + 1 - ylo, (1 - yhi) * 2 + ylo, (1 - yhi) * 2 + 1 - ylo]

    y_up, y_down = lax.rem(y + 1, 4), lax.rem(y + 3, 4)

    def a_copy(hd, yy, i, to_y):
        return remote(a_slot(hd, yy), a_slot(hd, yy), a_ss.at[hd, i], a_rs.at[hd, yy], device(pool, x, to_y, h, t))

    def a_copies(hd):
        return [a_copy(hd, y, 0, y_up), a_copy(hd, y, 1, y_down)]

    def a_arrival(hd, yy):
        return remote(a_slot(hd, yy), a_slot(hd, yy), a_ss.at[hd, 0], a_rs.at[hd, yy], z_partner)

    pl.semaphore_wait(barrier, len(friends))
    w_first = w_direct(0)
    for copy in w_over + w_first:
        copy.start()
    load_q.wait()
    for hd in range(KVL):
        for g in range(GROUP_HEADS):
            qs[hd, head_rows(g), :] = q_ref[:, head_cols(hd, g)]
    load_sk.wait()
    span_scores(0)
    for copy in load_k:
        copy.wait()
    pl.loop(0, BLOCKS)(lambda j: scores(0, j))
    load_v.wait()
    load_sv.wait()
    for hd in range(KVL):
        va[hd, :, :HD] = v_ref[:, hd * HD : (hd + 1) * HD]
        va[hd, :, HD:] = jnp.ones((PREFIX, HD), jnp.bfloat16)
        vas[hd, :, :HD] = sv_ref[:, hd * HD : (hd + 1) * HD]
        vas[hd, :, HD:] = jnp.ones((SPAN, HD), jnp.bfloat16)
    finish_max(0)
    span_weigh(0)
    span_scores(1)

    def middle(j):
        weigh(0, j)
        scores(1, j)

    pl.loop(0, BLOCKS)(middle)
    attended(0)
    first_a = a_copies(0)
    for copy in first_a:
        copy.start()
    w_first += pass_on(0)
    finish_max(1)
    span_weigh(1)
    pl.loop(0, BLOCKS)(lambda j: weigh(1, j))
    attended(1)
    second_a = a_copies(1)
    for copy in second_a:
        copy.start()

    load_res.wait()

    @pl.when(zero_pool)
    def _():
        for s in range(4):
            rows = res_ref[s * (SPAN // 4) : (s + 1) * (SPAN // 4), :].astype(jnp.float32)
            for k in range(4):
                put(s, every_fourth(k), rows[:, k * PIECE : (k + 1) * PIECE])

    @pl.when(jnp.logical_not(zero_pool))
    def _():
        for s in range(4):
            put(s, every, res_ref[:, s * PIECE : (s + 1) * PIECE].astype(jnp.float32))

    for s in range(4):
        rp[s] = get(s, every).astype(jnp.bfloat16)
        keeps, near, far = res_copies(s)

        @pl.when(keeps)
        def _():
            near.start()

        @pl.when(jnp.logical_not(keeps))
        def _():
            far.start()

    w_second = w_direct(1)
    for part in range(2):
        w_wait(1 - h, x, part)
        for copy in w_second[2 * part : 2 * part + 2]:
            copy.start()
    a_arrival(1, y_up).wait_recv()
    pass_second = a_copy(1, y_up, 2, y_down)
    pass_second.start()
    a_arrival(0, y_down).wait_recv()
    pass_first = a_copy(0, y_down, 2, y_up)
    pass_first.start()

    t1 = t + 1 - 2 * lax.rem(t, 2)
    t2 = lax.rem(t + 2, 4)
    t3 = 3 - t
    tpar = lax.rem(t, 2)
    thi = lax.div(t, 2)

    def piece_rows(piece):
        return pl.ds(pl.multiple_of(piece * WCOLS, WCOLS), WCOLS)

    def p1_copy(u, i, piece):
        return remote(
            pb.at[u, piece_rows(piece)], rcv1.at[lax.div(piece, 2), u], p1_ss.at[u, i],
            p1_rs.at[lax.div(piece, 2), u], device(pool, x, y, h, t1),
        )

    def p1_arrival(jj, u):
        return remote(rcv1.at[jj, u], rcv1.at[jj, u], p1_ss.at[u, 0], p1_rs.at[jj, u], z_partner)

    def p2_copy(u):
        return remote(s2.at[u], rcv2.at[u], p2_ss.at[u], p2_rs.at[u], device(pool, x, y, h, t2))

    def unit(u):
        hh = h if u < 2 else 1 - h
        pair = yhi if u % 2 == 0 else 1 - yhi
        rows = pl.ds(pl.multiple_of(pair * 2 * SPAN, 2 * SPAN), 2 * SPAN)
        total = nt(wg[hh, :, :HALF], ag[0, rows, :]) + nt(wg[hh, :, HALF:], ag[1, rows, :])
        pr[u] = total
        pb[u] = total.astype(jnp.bfloat16)
        copy = p1_copy(u, 0, t3)
        copy.start()
        return copy

    def last_part(u):
        copy = p1_copy(u, 1, t1)
        copy.start()
        return copy

    def second(u):
        p1_arrival(1 - thi, u).wait_recv()
        total = pr[u, piece_rows(t2), :] + rcv1[1 - thi, u].astype(jnp.float32)
        s2[u] = total.astype(jnp.bfloat16)
        copy = p2_copy(u)
        copy.start()
        return copy

    p1_sent = []
    p2_sent = []
    own_w.wait()
    w_rest(h)
    first_head = jnp.where(ylo == 0, 0, 1)
    a_arrival(first_head, y_partners[0]).wait_recv()
    p1_sent.append(unit(0))
    p1_sent.append(last_part(0))
    w_second += pass_on(1)
    a_arrival(1 - first_head, y_partners[2]).wait_recv()
    for hd in range(KVL):
        a_arrival(hd, y_partners[1]).wait_recv()
    p1_sent.append(unit(1))
    p2_sent.append(second(0))
    p1_sent.append(last_part(1))
    p2_sent.append(second(1))

    for pair in range(2):
        for a in range(2):
            at = pair * 2 + a
            pltpu.make_async_copy(rres.at[at], rres.at[at], res_rs.at[at]).wait()
        both = jnp.concatenate([rres[pair * 2], rres[pair * 2 + 1]], axis=0).astype(jnp.float32)
        blank = jnp.zeros((2 * SPAN, 3 * HD - PIECE), jnp.float32)
        rt[pair] = jnp.transpose(jnp.concatenate([both, blank], axis=1))

    w_rest(1 - h)
    p1_sent.append(unit(2))
    p1_sent.append(unit(3))
    p2_sent.append(second(2))
    p1_sent.append(last_part(2))
    p2_sent.append(second(3))
    p1_sent.append(last_part(3))

    def final_copy(s, slot_from, index):
        to_y = jnp.where(zero_pool, s, lax.div(s, 2) * 2 + yhi)
        to_h = jnp.where(zero_pool, h, ylo)
        slot = jnp.where(zero_pool, y, lax.rem(s, 2) * 2 + h)
        return remote(
            lb.at[slot_from], st.at[slot], f_ss.at[index], f_rs.at[slot],
            device(1 - pool, x, to_y, to_h, t),
        )

    def detour(s, slot_from, index):
        to_y = lax.div(s, 2) * 2 + yhi
        crosses = jnp.logical_and(jnp.logical_not(zero_pool), h != ylo)
        part = lax.rem(s, 2)
        copy = remote(
            lb.at[slot_from], mid.at[part], f_ss.at[index], g_rs.at[part],
            device(pool, x, to_y, h, t),
        )
        return jnp.logical_and(crosses, to_y != y), copy

    carries = jnp.logical_and(jnp.logical_not(zero_pool), ylo * 2 + 1 - h != y)

    def carried(a):
        return remote(
            mid.at[a], st.at[a * 2 + h], g_ss.at[a], f_rs.at[a * 2 + h],
            device(1 - pool, x, y, 1 - h, t),
        )

    turn[pl.ds(PIECE, 64), :] = jnp.zeros((64, 2 * SPAN), jnp.float32)
    own_index = y * 4 + t
    final_sent = []
    sum_sent = []
    for pp in range(2):
        pair = yhi if pp == 0 else 1 - yhi
        squares = jnp.zeros((1, 2 * SPAN), jnp.float32)
        for hh in range(2):
            u = hh * 2 + pp
            at = h if hh == 0 else 1 - h
            p1_arrival(thi, u).wait_recv()
            p2_copy(u).wait_recv()
            rows = pl.ds(pl.multiple_of(at * WCOLS, WCOLS), WCOLS)
            total = (
                pr[u, piece_rows(t), :]
                + rcv1[thi, u].astype(jnp.float32)
                + rcv2[u].astype(jnp.float32)
                + rt[pair, rows, :]
            )
            total = total.astype(jnp.bfloat16).astype(jnp.float32)
            turn[rows, :] = total
            squares = squares + jnp.sum(total * total, axis=0, keepdims=True)
        sums[own_index, pl.ds(pair, 1), :] = squares
        if pp == 1:
            for k, (yy, tt) in enumerate(peers):
                copy = remote(
                    sums.at[own_index], sums.at[own_index], q_ss.at[k], q_rs.at[own_index],
                    device(pool, x, yy, h, tt),
                )
                copy.start()
                sum_sent.append(copy)
        whole = jnp.transpose(turn[...])[:, :PIECE].astype(jnp.bfloat16)
        for a in range(2):
            lb[pp * 2 + a] = whole[a * SPAN : (a + 1) * SPAN]
            copy = final_copy(pair * 2 + a, pp * 2 + a, pp * 2 + a)
            hops, around = detour(pair * 2 + a, pp * 2 + a, pp * 2 + a)

            @pl.when(hops)
            def _():
                around.start()

            @pl.when(jnp.logical_not(hops))
            def _():
                copy.start()

            final_sent.append(copy)

    @pl.when(carries)
    def _():
        for a in range(2):
            remote(mid.at[a], mid.at[a], g_ss.at[a], g_rs.at[a], z_partner).wait_recv()
            carried(a).start()

    total = sums[own_index]
    for k, (yy, tt) in enumerate(peers):
        index = yy * 4 + tt
        remote(sums.at[index], sums.at[index], q_ss.at[k], q_rs.at[index], z_partner).wait_recv()
        total = total + sums[index]
    mean[...] = total * (1.0 / D)
    for b in range(2):
        copy = remote(mean, means.at[h], m_ss.at[b], m_rs.at[h], device(1 - pool, x, y, b, t))
        copy.start()
        sum_sent.append(copy)

    for s in range(4):
        remote(lb.at[s], st.at[s], f_ss.at[s], f_rs.at[s], z_partner).wait_recv()
        put(s, every, st[s].astype(jnp.float32))

    def lay_out(at):
        @pl.when(zero_pool)
        def _():
            for s in range(4):
                quarter = [get(s, every_fourth(k)) for k in range(4)]
                tiles[at, s * (SPAN // 4) : (s + 1) * (SPAN // 4), :] = jnp.concatenate(
                    quarter, axis=1
                ).astype(jnp.bfloat16)

        @pl.when(jnp.logical_not(zero_pool))
        def _():
            tiles[at] = jnp.concatenate([get(s, every) for s in range(4)], axis=1).astype(jnp.bfloat16)

    lay_out(0)
    stream_out = pltpu.make_async_copy(tiles.at[0], stream_hbm.at[0], out_sem.at[0])
    stream_out.start()
    gains = [gain_ref[:, r * PIECE : (r + 1) * PIECE] for r in range(4)]

    def gain_at(s):
        return jnp.where(zero_pool, ylo * 2 + h, s)

    blank = jnp.zeros((1, 3 * HD - PIECE), jnp.float32)
    sub = lax.broadcasted_iota(jnp.int32, (8, 2 * SPAN), 0)
    scales = []
    for b in range(2):
        remote(mean, means.at[b], m_ss.at[b], m_rs.at[b], z_partner).wait_recv()
        scales.append(lax.rsqrt(means[b] + EPSILON))
    for s in range(4):
        from_h = jnp.where(zero_pool, s % 2, h)
        from_a = jnp.where(zero_pool, s // 2, ylo)
        picked = jnp.where(from_h == 0, scales[0], scales[1])
        row = jnp.sum(jnp.where(sub == yhi, picked, 0.0), axis=0, keepdims=True)
        row = jnp.where(from_a == 0, row[:, : 2 * HD], row[:, 2 * SPAN - 2 * HD :])
        turned = jnp.transpose(jnp.broadcast_to(row, (HD, 2 * HD)))
        wide = jnp.where(from_a == 0, turned[:SPAN], turned[2 * HD - SPAN :])
        gain = gains[0]
        for r in range(4):
            gain = jnp.where(gain_at(s) == r, gains[r], gain)
        gain = jnp.concatenate([gain, blank], axis=1)
        for c in range(3):
            p32[s, c] = p32[s, c] * wide * gain[:, c * HD : (c + 1) * HD]
    lay_out(1)
    normed_out = pltpu.make_async_copy(tiles.at[1], normed_hbm.at[0], out_sem.at[1])
    normed_out.start()

    @pl.when(carries)
    def _():
        for a in range(2):
            carried(a).wait_send()

    for copy in w_over + [pass_first, pass_second] + w_first + w_second + first_a + second_a + p1_sent + p2_sent + final_sent + sum_sent:
        copy.wait_send()
    for s in range(4):
        keeps, near, far = res_copies(s)

        @pl.when(jnp.logical_not(keeps))
        def _():
            far.wait_send()

    stream_out.wait()
    normed_out.wait()


def fused(plen, slen, q, k, v, sk, sv, res, w, gain):
    smem = pl.BlockSpec(memory_space=pltpu.SMEM)
    vmem = pl.BlockSpec(memory_space=pltpu.VMEM)
    hbm = pl.BlockSpec(memory_space=pl.ANY)
    dma = pltpu.SemaphoreType.DMA
    bf, f32 = jnp.bfloat16, jnp.float32
    out = jax.ShapeDtypeStruct((1, SPAN, 2 * HALF), bf)
    return pl.pallas_call(
        body,
        out_shape=(out, out),
        in_specs=[smem, smem] + [hbm] * 7 + [vmem],
        out_specs=(hbm, hbm),
        scratch_shapes=[
            pltpu.VMEM((SPAN, 2 * HALF), bf),
            pltpu.VMEM((PREFIX, KVL * HD), bf),
            pltpu.VMEM((PREFIX, KVL * HD), bf),
            pltpu.VMEM((SPAN, KVL * HD), bf),
            pltpu.VMEM((SPAN, KVL * HD), bf),
            pltpu.VMEM((SPAN, 2 * HALF), bf),
            pltpu.VMEM((4, 3, SPAN, HD), f32),
            pltpu.VMEM((4, SPAN, PIECE), bf),
            pltpu.VMEM((2, SPAN, 2 * HALF), bf),
            pltpu.VMEM((KVL, ROWS, HD), bf),
            pltpu.VMEM((3, ROWS, KEY_BLOCK), f32),
            pltpu.VMEM((KVL, ROWS, SPAN), f32),
            pltpu.VMEM((KVL, ROWS, HD), f32),
            pltpu.VMEM((KVL, ROWS, 2 * HD), f32),
            pltpu.VMEM((KVL, PREFIX, 2 * HD), bf),
            pltpu.VMEM((KVL, SPAN, 2 * HD), bf),
            pltpu.VMEM((2, 4 * WCOLS, 2 * HALF), bf),
            pltpu.VMEM((KVL, 4 * SPAN, HALF), bf),
            pltpu.VMEM((4, 4 * WCOLS, 2 * SPAN), f32),
            pltpu.VMEM((4, 4 * WCOLS, 2 * SPAN), bf),
            pltpu.VMEM((2, 4, WCOLS, 2 * SPAN), bf),
            pltpu.VMEM((4, WCOLS, 2 * SPAN), bf),
            pltpu.VMEM((4, WCOLS, 2 * SPAN), bf),
            pltpu.VMEM((4, SPAN, PIECE), bf),
            pltpu.VMEM((2, PIECE + 64, 2 * SPAN), f32),
            pltpu.VMEM((PIECE + 64, 2 * SPAN), f32),
            pltpu.VMEM((4, SPAN, PIECE), bf),
            pltpu.VMEM((4, SPAN, PIECE), bf),
            pltpu.VMEM((2, SPAN, PIECE), bf),
            pltpu.VMEM((16, 8, 2 * SPAN), f32),
            pltpu.VMEM((8, 2 * SPAN), f32),
            pltpu.VMEM((2, 8, 2 * SPAN), f32),
            dma((5 + BLOCKS,)),
            dma,
            dma((2,)),
            dma((2, 2, 3)),
            dma((2, 4, 2)),
            dma((KVL, 3)),
            dma((KVL, 4)),
            dma((4,)),
            dma((4,)),
            dma((4, 2)),
            dma((2, 4)),
            dma((4,)),
            dma((4,)),
            dma((4,)),
            dma((4,)),
            dma((2,)),
            dma((2,)),
            dma((16,)),
            dma((16,)),
            dma((2,)),
            dma((2,)),
            dma((2,)),
        ],
        compiler_params=pltpu.CompilerParams(
            has_side_effects=True, collective_id=0, vmem_limit_bytes=62 << 20
        ),
        name="fused",
    )(plen, slen, q, k, v, sk, sv, res, w, gain)


def copy_body(a, b, out_a, out_b):
    out_a[...] = a[...]
    out_b[...] = b[...]


def hand_over(stream, normed):
    block = pl.BlockSpec((1, SPAN // 2, 2 * HALF), lambda i: (0, i, 0))
    out = jax.ShapeDtypeStruct(stream.shape, stream.dtype)
    return pl.pallas_call(
        copy_body, grid=(2,), out_shape=(out, out), in_specs=[block, block],
        out_specs=(block, block), name="hand_over",
    )(stream, normed)


def shards(
    queries, new_keys, new_values, cache_keys, cache_values, prefix_len, span_len, residual, out_proj,
    norm_gain,
):
    return hand_over(*fused(
        prefix_len, span_len, queries[0], cache_keys[0, 0], cache_values[0, 0], new_keys[0],
        new_values[0], residual[0], jnp.swapaxes(out_proj[0], 0, 1), norm_gain,
    ))


def solution(mesh):
    placed = (
        P("pool", "group", "tensor"),
        P("pool", "group", "tensor"),
        P("pool", "group", "tensor"),
        P("pool", "group", None, "tensor"),
        P("pool", "group", None, "tensor"),
        P("pool", "group"),
        P("pool", "group"),
        P("pool", "group", "tensor"),
        P("pool", "tensor", "group"),
        P("pool", "tensor"),
    )
    return jax.shard_map(
        shards,
        mesh=mesh,
        in_specs=placed,
        out_specs=(P("pool", "group", "tensor"), P("pool", "group", "tensor")),
        check_vma=False,
    )
```
